256 devices in a mesh: ctx: 64 (over z, y, core), head: 4 (over x).
Axes of the slice: x: 4, y: 4, z: 8, core: 2. Of those that a mesh axis runs over, the one named last changes fastest.
Arguments:
- query_act: bfloat16 [16384, 4096], P('ctx', 'head'), may hold values from -6 to 6
- key_act: bfloat16 [16384, 4096], P('ctx', 'head'), may hold values from -6 to 6
- value_act: bfloat16 [16384, 4096], P('ctx', 'head'), may hold values from -6 to 6
- out_weight: bfloat16 [3072, 4096], P('ctx', 'head'), may hold values from -0.09375 to 0.09375
- out_cotangent: bfloat16 [16384, 3072], P('ctx', 'head'), may hold values from -16 to 16
Outputs:
- grad_query: bfloat16 [16384, 4096], P('ctx', 'head')
- grad_key: bfloat16 [16384, 4096], P('ctx', 'head')
- grad_value: bfloat16 [16384, 4096], P('ctx', 'head')
- grad_weight: float32 [3072, 4096], P('ctx', 'head')
The draws below stay inside these ranges and needn't reach their ends.
All inputs are finite; a program needn't handle non-finite values.
Results may differ from the reference program's by a relative error of at most 0.014.
Values may be sent and summed in bfloat16 or wider, within the bound.
A program may use at most 128 MiB of HBM per device.

```python
import jax
import jax.numpy as jnp
from jax import lax

D = 3072
HDIM = 128
HEADS = 32
BLK = 256
TOKENS = 16384


def with_spikes(drawn, key, source, target, blocks, factor):
    owner, partner = [(jnp.arange(drawn.shape[position]) // (drawn.shape[position] // blocks)).reshape([-1 if axis == position else 1 for axis in range(drawn.ndim)]) for position in (source, target)]
    chosen = jax.random.permutation(key, blocks)[partner]
    strong = (owner == chosen) | (owner == (partner + blocks // 2) % blocks)
    return jnp.where(strong, factor * drawn, drawn)


def level_of(key, shape, split, smallest, high):
    level, own = 1.0, jax.random.fold_in(key, 6)
    for position, shards_of in split:
        heights = jnp.exp(jax.random.uniform(jax.random.fold_in(own, position), (shards_of,), jnp.float32, smallest / len(split), high / len(split)))
        level = level * jnp.repeat(heights, shape[position] // shards_of).reshape([-1 if axis == position else 1 for axis in range(len(shape))])
    return level


def centred(own_key, extent, spread, limit, cuts=(), held_as=jnp.bfloat16):
    array = jax.random.normal(own_key, extent, jnp.float32) * spread
    if len(cuts) > 0:
        array = level_of(own_key, extent, cuts, -0.22, 0.18) * array
    return jnp.clip(array, min=-limit, max=limit).astype(held_as)


def noise_with(key, extent, deviation, bound, split, heavy, held_as=jnp.bfloat16):
    values = deviation * jax.random.normal(key, extent, jnp.float32)
    if split:
        values = values * level_of(key, extent, split, -0.22, 0.18)
    return jnp.clip(with_spikes(values, jax.random.fold_in(key, 3), *heavy), -bound, bound).astype(held_as)


def setup_inputs(seed: int = 0) -> dict:
    arg_keys = jax.random.split(jax.random.key(seed), 6)
    return {
        "query_act": centred(arg_keys[0], (TOKENS, HEADS * HDIM), 1.0, 6.0, ((0, 64), (1, 4))),
        "key_act": centred(arg_keys[1], (TOKENS, HEADS * HDIM), 1.0, 6.0, ((0, 64), (1, 4))),
        "value_act": centred(arg_keys[2], (TOKENS, HEADS * HDIM), 1.0, 6.0, ((0, 64), (1, 4))),
        "out_weight": centred(arg_keys[3], (D, HEADS * HDIM), (HEADS * HDIM) ** -0.5, 0.09375, ((0, 64), (1, 4))),
        "out_cotangent": noise_with(arg_keys[4], (TOKENS, D), 1.0, 16.0, ((0, 64), (1, 4)), (0, 1, 64, 4.0)),
    }


EPS = 1e-06

def head_grads(pieces):
    q, k, v, da = pieces
    nb = TOKENS // BLK
    q = q.reshape(nb, BLK, HDIM).astype(jnp.float32)
    k = k.reshape(nb, BLK, HDIM).astype(jnp.float32)
    v = v.reshape(nb, BLK, HDIM).astype(jnp.float32)
    da = da.reshape(nb, BLK, HDIM)
    block_kv = jnp.einsum('bti,btj->bij', k, v)
    prior = (jnp.cumsum(block_kv, axis=0) - block_kv).astype(jnp.bfloat16).astype(jnp.float32)
    mask = jnp.tril(jnp.ones((BLK, BLK), jnp.float32))
    scores = (jnp.einsum('bti,bsi->bts', q, k) * mask).astype(jnp.bfloat16).astype(jnp.float32)
    raw = jnp.einsum('bts,bsj->btj', scores, v) + jnp.einsum('bti,bij->btj', q, prior)
    inv_rms = lax.rsqrt(lax.optimization_barrier(jnp.mean(raw * raw, axis=-1, keepdims=True)) + EPS)
    normal = raw * inv_rms
    normed = normal.astype(jnp.bfloat16)
    center = lax.optimization_barrier(jnp.mean(da * normal, axis=-1, keepdims=True))
    d_raw = (inv_rms * (da - normal * center)).astype(jnp.bfloat16).astype(jnp.float32)
    block_g = jnp.einsum('bti,btj->bij', q, d_raw)
    later = (lax.optimization_barrier(jnp.sum(block_g, axis=0)) - jnp.cumsum(block_g, axis=0)).astype(jnp.bfloat16).astype(jnp.float32)
    d_scores = (jnp.einsum('btj,bsj->bts', d_raw, v) * mask).astype(jnp.bfloat16).astype(jnp.float32)
    grad_q = jnp.einsum('bts,bsi->bti', d_scores, k) + jnp.einsum('btj,bij->bti', d_raw, prior)
    grad_k = jnp.einsum('bts,bti->bsi', d_scores, q) + jnp.einsum('bsj,bij->bsi', v, later)
    grad_v = jnp.einsum('bts,btj->bsj', scores, d_raw) + jnp.einsum('bsi,bij->bsj', k, later)
    shape = (TOKENS, HDIM)
    return (grad_q.reshape(shape).astype(jnp.bfloat16), grad_k.reshape(shape).astype(jnp.bfloat16), grad_v.reshape(shape).astype(jnp.bfloat16), normed.reshape(shape))

def by_head(x):
    return jnp.transpose(x.reshape(TOKENS, HEADS, HDIM), (1, 0, 2))

def back(x):
    return jnp.transpose(x, (1, 0, 2)).reshape(TOKENS, HEADS * HDIM)

def reference(query_act, key_act, value_act, out_weight, out_cotangent):
    d_attn = jnp.dot(out_cotangent, out_weight, preferred_element_type=jnp.float32)
    grad_q, grad_k, grad_v, normed = lax.map(head_grads, (by_head(query_act), by_head(key_act), by_head(value_act), by_head(d_attn)))
    normed = back(normed)
    grad_weight = jnp.dot(out_cotangent.T, normed, preferred_element_type=jnp.float32) * (1.0 / jnp.sqrt(jnp.float32(TOKENS)))
    return (back(grad_q), back(grad_k), back(grad_v), grad_weight)
```

```python
import functools

import jax
import jax.numpy as jnp
from jax import lax
from jax.experimental import pallas as pl
from jax.experimental.pallas import tpu as pltpu
from jax.sharding import Mesh
from jax.sharding import PartitionSpec as P

HDIM = 128
BLK = 256
EPS = 1e-06
NZ, NY, NC, NX = 8, 4, 2, 4
HEADS = 8
ROWS = 48
WIDTH = 1024
COLS = 768
SLAB = NY * NC * ROWS
PA = 16
PB = 32
F32 = jnp.float32
BF16 = jnp.bfloat16
GRADW_SCALE = 1.0 / 128.0


def dot_nn(a, b):
    return lax.dot_general(a, b, (((1,), (0,)), ((), ())), preferred_element_type=F32)


def dot_nt(a, b):
    return lax.dot_general(a, b, (((1,), (1,)), ((), ())), preferred_element_type=F32)


def dot_tn(a, b):
    return lax.dot_general(a, b, (((0,), (0,)), ((), ())), preferred_element_type=F32)


def kernel(
    q_hbm, k_hbm, v_hbm, w_hbm, cot_hbm,
    gq_ref, gk_ref, gv_ref, gw_ref,
    q, k, v, wb, cot, cot_t, cot_t_sib, normed, normed_sib, scores, raw, inv, da, draw, pk, pv,
    part, st1, r1, st2, r2, red, zst, zr, qst, qr, qy1s, qy1r, qy2s, qy2r,
    s_send, a_recv, a_pre, b_tot, b1_recv, b_base, b2_recv, c_send, c_recv,
    load_sem, cx1, cx2, zp_sem, yp1, yp2, qy1, qy2, zq, sib, tsib, nsib,
    ry1, ry2, rz, qz, qya, qyb, sa, sb1, sb2, sc,
):
    z, y, c, x = (lax.axis_index(n) for n in ("z", "y", "c", "x"))
    up_z, dn_z = lax.rem(z + 1, NZ), lax.rem(z + NZ - 1, NZ)
    up_y, dn_y, far_y = lax.rem(y + 1, NY), lax.rem(y + 3, NY), lax.rem(y + 2, NY)
    up_x, dn_x, far_x = lax.rem(x + 1, NX), lax.rem(x + 3, NX), lax.rem(x + 2, NX)
    other = 1 - c
    plane = y * 2 + c
    zdir = ({"z": up_z}, {"z": dn_z})
    ydir = ({"y": up_y}, {"y": dn_y})
    xdir = ({"x": up_x}, {"x": dn_x})
    pending = []

    def send(src, dst, sems, at, device):
        copy = pltpu.make_async_remote_copy(
            src_ref=src, dst_ref=dst, send_sem=sems.at[(0, *at)], recv_sem=sems.at[(1, *at)],
            device_id=device, device_id_type=pl.DeviceIdType.MESH,
        )
        copy.start()
        pending.append(copy)
        return copy

    loads = [
        pltpu.make_async_copy(src, dst, load_sem.at[i])
        for i, (src, dst) in enumerate(
            ((cot_hbm, cot.at[x]), (w_hbm, wb.at[z, y, c]), (k_hbm, k), (v_hbm, v), (q_hbm, q))
        )
    ]
    for load in loads:
        load.start()

    def plane_peer(o):
        j = lax.rem(plane + o, 8)
        return j, {"y": lax.div(j, 2), "c": lax.rem(j, 2)}

    peers = [plane_peer(o)[1] for o in range(1, 8)]
    peers += [{"z": lax.rem(z + o, NZ)} for o in range(1, NZ)]
    peers += list(xdir)
    barrier = pltpu.get_barrier_semaphore()
    for peer in peers:
        pl.semaphore_signal(barrier, inc=1, device_id=peer, device_id_type=pl.DeviceIdType.MESH)
    pl.semaphore_wait(barrier, len(peers))

    loads[0].wait()
    cot1 = [send(cot.at[x], cot.at[x], cx1, (d,), xdir[d]) for d in (0, 1)]
    cot2 = []

    def cot_forward():
        cot1[0].wait_recv()
        half = cot.at[dn_x, pl.ds(0, 128)]
        cot2.append(send(half, half, cx2, (0,), xdir[0]))
        cot1[1].wait_recv()
        half = cot.at[up_x, pl.ds(128, 128)]
        cot2.append(send(half, half, cx2, (1,), xdir[1]))

    ag_z = [lax.rem(z + NZ + o, NZ) for o in (0, -1, 1, -2, 2, -3, 3, 4)]
    zp_c, yp1_c, yp2_c, qy1_c, qy2_c, zq_c, sib_c = {}, {}, {}, {}, {}, {}, {}

    def send_zp(r):
        for d, org in ((0, lax.rem(z + NZ - r, NZ)), (1, lax.rem(z + r, NZ))):
            rows = pl.ds(0, PB) if r < 3 else pl.ds(PA * d, PA)
            blk = wb.at[org, y, c, rows]
            zp_c[d, r] = send(blk, blk, zp_sem, (d, r), zdir[d])

    def send_yp1(i):
        for d in (0, 1):
            blk = wb.at[ag_z[i], y, c, pl.ds(0, PB)]
            yp1_c[d, i] = send(blk, blk, yp1, (d, i), ydir[d])

    def forward_yp(i):
        for d, org in ((0, dn_y), (1, up_y)):
            yp1_c[d, i].wait_recv()
            blk = wb.at[ag_z[i], org, c, pl.ds(PA * d, PA)]
            yp2_c[d, i] = send(blk, blk, yp2, (d, i), ydir[d])

    def send_qy1():
        for d in (0, 1):
            blk = wb.at[z, y, c, pl.ds(PB, PA)]
            qy1_c[d] = send(blk, blk, qy1, (d,), ydir[d])

    def forward_qy():
        for d, org in ((0, dn_y), (1, up_y)):
            qy1_c[d].wait_recv()
            blk = wb.at[z, org, c, pl.ds(PB, PA), pl.ds(512 * d, 512)]
            qy2_c[d] = send(blk, blk, qy2, (d,), ydir[d])

    def send_zq(r):
        for d, org in ((0, lax.rem(z + NZ - r, NZ)), (1, lax.rem(z + r, NZ))):
            ys = pl.ds(0, NY) if r < 3 else pl.ds(2 * d, 2)
            blk = wb.at[org, ys, c, pl.ds(PB, PA)]
            zq_c[d, r] = send(blk, blk, zq, (d, r), zdir[d])

    def recv_both(copies, r):
        for d in (0, 1):
            copies[d, r].wait_recv()

    def send_sib(i):
        recv_both(yp2_c, i)
        blk = wb.at[ag_z[i], :, c]
        sib_c[i] = send(blk, blk, sib, (i,), {"c": other})

    def ag0():
        send_zp(0)
        send_qy1()
        send_yp1(0)

    def ag1():
        recv_both(zp_c, 0)
        send_zp(1)
        send_yp1(1)
        send_yp1(2)
        forward_qy()
        forward_yp(0)
        qy2_c[0].wait_recv()
        qy2_c[1].wait_recv()
        send_zq(0)

    def ag2():
        recv_both(zp_c, 1)
        send_zp(2)
        send_yp1(3)
        send_yp1(4)
        recv_both(zq_c, 0)
        send_zq(1)
        forward_yp(1)
        forward_yp(2)
        send_sib(0)

    def ag3():
        recv_both(zp_c, 2)
        send_zp(3)
        send_yp1(5)
        send_yp1(6)
        recv_both(zq_c, 1)
        send_zq(2)
        forward_yp(3)
        forward_yp(4)
        send_sib(1)
        send_sib(2)

    def ag4():
        recv_both(zp_c, 3)
        send_yp1(7)
        recv_both(zq_c, 2)
        send_zq(3)
        forward_yp(5)
        forward_yp(6)
        send_sib(3)
        send_sib(4)

    def ag5():
        forward_yp(7)
        send_sib(5)
        send_sib(6)
        recv_both(zq_c, 3)
        send_sib(7)

    class Scan:
        def __init__(self, s):
            self.s = s
            self.order = (range(8), range(7, -1, -1))[s]

        def start(self):
            s = self.s
            self.a = []
            for o in range(1, 8):
                j, dev = plane_peer(o)
                self.a.append(send(s_send.at[s, j], a_recv.at[s, plane], sa, (s, o), dev))
            a_recv[s, plane] = s_send[s, plane]

        def a_done(self):
            s = self.s
            for copy in self.a:
                copy.wait_recv()
            run = jnp.zeros((HDIM, HDIM), F32)
            for j in self.order:
                a_pre[s, j] = run
                run = run + a_recv[s, j].astype(F32)
            b_tot[s] = run.reshape(NZ, 16, HDIM)
            self.b1 = []
            for o in range(1, NZ):
                t = lax.rem(z + o, NZ)
                self.b1.append(send(b_tot.at[s, t], b1_recv.at[s, z], sb1, (s, o), {"z": t}))
            b1_recv[s, z] = b_tot[s, z]

        def b1_done(self):
            s = self.s
            for copy in self.b1:
                copy.wait_recv()
            run = jnp.zeros((16, HDIM), F32)
            for t in self.order:
                b_base[s, t] = run
                run = run + b1_recv[s, t]
            self.b2 = []
            for o in range(1, NZ):
                t = lax.rem(z + o, NZ)
                self.b2.append(send(b_base.at[s, t], b2_recv.at[s, z], sb2, (s, o), {"z": t}))
            b2_recv[s, z] = b_base[s, z]

        def b2_done(self):
            s = self.s
            for copy in self.b2:
                copy.wait_recv()
            base = b2_recv[s].reshape(HDIM, HDIM)
            for j in range(8):
                c_send[s, j] = (base + a_pre[s, j]).astype(BF16)
            self.c = []
            for o in range(1, 8):
                j, dev = plane_peer(o)
                self.c.append(send(c_send.at[s, j], c_recv.at[s, plane], sc, (s, o), dev))
            c_recv[s, plane] = c_send[s, plane]

        def c_done(self):
            for copy in self.c:
                copy.wait_recv()

    kv_scan, g_scan = Scan(0), Scan(1)

    def cols_of(h):
        return pl.ds(pl.multiple_of(h * HDIM, HDIM), HDIM)

    def for_heads(first, count, fn, unroll=2):
        @pl.loop(0, count // unroll)
        def _(i):
            for u in range(unroll):
                fn(first + i * unroll + u)

    mask = (
        lax.broadcasted_iota(jnp.int32, (BLK, BLK), 0)
        >= lax.broadcasted_iota(jnp.int32, (BLK, BLK), 1)
    )

    def kv_head(h):
        cs = cols_of(h)
        s_send[0, h] = dot_tn(k[:, cs], v[:, cs]).astype(BF16)

    def score_head(h):
        cs = cols_of(h)
        s = jnp.where(mask, dot_nt(q[:, cs], k[:, cs]), 0.0).astype(BF16)
        scores[h] = s
        raw[:, cs] = dot_nn(s, v[:, cs])

    def norm_head(h):
        cs = cols_of(h)
        r = raw[:, cs] + dot_nn(q[:, cs], c_recv[0, h])
        i = lax.rsqrt(jnp.mean(r * r, axis=-1, keepdims=True) + EPS)
        a = r * i
        raw[:, cs] = a
        inv[h] = i
        normed[:, cs] = a.astype(BF16)

    def draw_head(h):
        cs = cols_of(h)
        d, a = da[:, cs], raw[:, cs]
        center = jnp.mean(d * a, axis=-1, keepdims=True)
        dr = (inv[h] * (d - a * center)).astype(BF16)
        draw[:, cs] = dr
        s_send[1, h] = dot_tn(q[:, cs], dr).astype(BF16)

    def local_grad_head(h):
        cs = cols_of(h)
        dr = draw[:, cs]
        ds = jnp.where(mask, dot_nt(dr, v[:, cs]), 0.0).astype(BF16)
        gq_ref[:, cs] = (dot_nn(ds, k[:, cs]) + dot_nt(dr, c_recv[0, h])).astype(BF16)
        pk[:, cs] = dot_tn(ds, q[:, cs])
        pv[:, cs] = dot_tn(scores[h], dr)

    def final_grad_head(h):
        cs = cols_of(h)
        gk_ref[:, cs] = (pk[:, cs] + dot_nt(v[:, cs], c_recv[1, h])).astype(BF16)
        gv_ref[:, cs] = (pv[:, cs] + dot_nn(k[:, cs], c_recv[1, h])).astype(BF16)

    x_order = (x, dn_x, up_x, far_x)
    tsib_c = {}

    def turn(i):
        xo = x_order[i]
        for half in (0, 1):
            t = cot[xo, :, pl.ds(half * SLAB, SLAB)].T
            cot_t[xo * 2 + half] = t.reshape(NY, NC, ROWS, BLK)
        src = cot_t.at[pl.ds(xo * 2, 2), :, other]
        tsib_c[i] = send(src, cot_t_sib.at[pl.ds(xo * 2, 2)], tsib, (i,), {"c": other})

    def d_attn(idx, first=False):
        for i in idx:
            sib_c[i].wait_recv()

        @pl.loop(0, 4)
        def _(n):
            cs = pl.ds(pl.multiple_of(n * 256, 256), 256)
            acc = None if first else da[:, cs]
            for i in idx:
                zo = ag_z[i]
                lanes = pl.ds(pl.multiple_of(lax.rem(zo, 2) * SLAB, 128), SLAB)
                t = dot_nn(cot[lax.div(zo, 2), :, lanes], wb[zo, :, :, :, cs].reshape(SLAB, 256))
                acc = t if acc is None else acc + t
            da[:, cs] = acc

    rs_z = [lax.rem(z + NZ + o, NZ) for o in (4, 3, -3, 2, -2, 1, -1, 0)]
    up_of, dn_of = (0, 1, 3, 5), (0, 2, 4, 6)
    ry1_c, ry2_c, rz_c, qz_c, qya_c, qyb_c = {}, {}, {}, {}, {}, {}

    def product(i):
        zt = rs_z[i]

        @pl.loop(0, 4)
        def _(n):
            cs = pl.ds(pl.multiple_of(n * 256, 256), 256)
            acc = dot_nn(cot_t[zt, :, c].reshape(NY * ROWS, BLK), normed[:, cs])
            acc = acc + dot_nn(cot_t_sib[zt].reshape(NY * ROWS, BLK), normed_sib[:, cs])
            part[zt, :, :, cs] = acc.reshape(NY, ROWS, 256)

    def step1(i):
        st1[i] = part[rs_z[i], far_y, 0:PB].astype(BF16)
        for d in (0, 1):
            ry1_c[d, i] = send(st1.at[i, pl.ds(PA * d, PA)], r1.at[d, i], ry1, (d, i), ydir[d])

    def step2(i):
        zt = rs_z[i]
        for d, t in ((0, up_y), (1, dn_y)):
            ry1_c[d, i].wait_recv()
            mine, rest = slice(PA * d, PA * d + PA), slice(PA - PA * d, PB - PA * d)
            st2[d, i, mine] = (part[zt, t, mine] + r1[d, i].astype(F32)).astype(BF16)
            st2[d, i, rest] = part[zt, t, rest].astype(BF16)
            ry2_c[d, i] = send(st2.at[d, i], r2.at[d, i], ry2, (d, i), ydir[d])

    def step3(i):
        recv_both(ry2_c, i)
        red[i] = part[rs_z[i], y, 0:PB] + (r2[0, i].astype(F32) + r2[1, i].astype(F32))

    def chain(s):
        for d, idx in ((0, up_of), (1, dn_of)):
            i = idx[s]
            mine = slice(PA * d, PA * d + PA)
            if s == 0:
                zst[d, 0, mine] = red[i, mine].astype(BF16)
                blk = pl.ds(PA * d, PA)
                rz_c[d, s] = send(zst.at[d, 0, blk], zr.at[d, 0, blk], rz, (d, s), zdir[d])
                continue
            rz_c[d, s - 1].wait_recv()
            if s == 1:
                rest = slice(PA - PA * d, PB - PA * d)
                zst[d, s, mine] = (red[i, mine] + zr[d, 0, mine].astype(F32)).astype(BF16)
                zst[d, s, rest] = red[i, rest].astype(BF16)
            else:
                zst[d, s] = (red[i] + zr[d, s - 1].astype(F32)).astype(BF16)
            rz_c[d, s] = send(zst.at[d, s], zr.at[d, s], rz, (d, s), zdir[d])

    def chain_end():
        recv_both(rz_c, 3)
        total = red[7] + (zr[0, 3].astype(F32) + zr[1, 3].astype(F32))
        gw_ref[0:PB] = total * GRADW_SCALE

    def qchain(s):
        for d, idx in ((0, up_of), (1, dn_of)):
            zt = rs_z[idx[s]]
            mine = slice(2 * d, 2 * d + 2)
            if s == 0:
                qst[d, 0, mine] = part[zt, mine, PB:ROWS].astype(BF16)
                blk = pl.ds(2 * d, 2)
                qz_c[d, s] = send(qst.at[d, 0, blk], qr.at[d, 0, blk], qz, (d, s), zdir[d])
                continue
            qz_c[d, s - 1].wait_recv()
            if s == 1:
                rest = slice(2 - 2 * d, 4 - 2 * d)
                got = qr[d, 0, mine].astype(F32)
                qst[d, s, mine] = (part[zt, mine, PB:ROWS] + got).astype(BF16)
                qst[d, s, rest] = part[zt, rest, PB:ROWS].astype(BF16)
            else:
                got = qr[d, s - 1].astype(F32)
                qst[d, s] = (part[zt, :, PB:ROWS] + got).astype(BF16)
            qz_c[d, s] = send(qst.at[d, s], qr.at[d, s], qz, (d, s), zdir[d])

    def q_y1():
        recv_both(qz_c, 3)
        part[z, :, PB:ROWS] = part[z, :, PB:ROWS] + (qr[0, 3].astype(F32) + qr[1, 3].astype(F32))
        for d in (0, 1):
            qy1s[d] = part[z, far_y, PB:ROWS, 512 * d : 512 * d + 512].astype(BF16)
            qya_c[d] = send(qy1s.at[d], qy1r.at[d], qya, (d,), ydir[d])

    def q_y2():
        for d, t in ((0, up_y), (1, dn_y)):
            qya_c[d].wait_recv()
            mine = slice(512 * d, 512 * d + 512)
            rest = slice(512 - 512 * d, 1024 - 512 * d)
            qy2s[d, :, mine] = (part[z, t, PB:ROWS, mine] + qy1r[d].astype(F32)).astype(BF16)
            qy2s[d, :, rest] = part[z, t, PB:ROWS, rest].astype(BF16)
            qyb_c[d] = send(qy2s.at[d], qy2r.at[d], qyb, (d,), ydir[d])

    def q_end():
        for d in (0, 1):
            qyb_c[d].wait_recv()
        total = part[z, y, PB:ROWS] + (qy2r[0].astype(F32) + qy2r[1].astype(F32))
        gw_ref[PB:ROWS] = total * GRADW_SCALE

    loads[1].wait()
    ag0()
    loads[2].wait()
    loads[3].wait()
    for_heads(0, 8, kv_head, 4)
    kv_scan.start()
    loads[4].wait()
    ag1()
    for_heads(0, 4, score_head)
    kv_scan.a_done()
    ag2()
    for_heads(4, 4, score_head)
    kv_scan.b1_done()
    turn(0)
    cot_forward()
    ag3()
    kv_scan.b2_done()
    turn(1)
    turn(2)
    ag4()
    kv_scan.c_done()
    for_heads(0, 8, norm_head)
    nsib_c = send(normed, normed_sib, nsib, (), {"c": other})
    for copy in cot2:
        copy.wait_recv()
    turn(3)
    ag5()
    d_attn((0, 1, 2), True)
    nsib_c.wait_recv()
    for i in range(4):
        tsib_c[i].wait_recv()
    for i in range(8):
        product(i)
        step1(i)
        if i == 0:
            qchain(0)
    d_attn((3, 4))
    d_attn((5, 6))
    qchain(1)
    d_attn((7,))
    for_heads(0, 8, draw_head)
    g_scan.start()
    for i in range(3):
        step2(i)
    qchain(2)
    g_scan.a_done()
    for i in range(3, 7):
        step2(i)
    step3(0)
    chain(0)
    for_heads(0, 4, local_grad_head)
    g_scan.b1_done()
    qchain(3)
    step2(7)
    step3(1)
    step3(2)
    chain(1)
    for_heads(4, 4, local_grad_head)
    g_scan.b2_done()
    step3(3)
    step3(4)
    chain(2)
    q_y1()
    g_scan.c_done()
    for_heads(0, 8, final_grad_head)
    step3(5)
    step3(6)
    chain(3)
    q_y2()
    step3(7)
    q_end()
    chain_end()
    for copy in pending:
        copy.wait_send()


def body(query_act, key_act, value_act, out_weight, out_cotangent):
    vm = pltpu.VMEM
    dma = pltpu.SemaphoreType.DMA
    scratch = [
        vm((BLK, WIDTH), BF16), vm((BLK, WIDTH), BF16), vm((BLK, WIDTH), BF16),
        vm((NZ, NY, NC, ROWS, WIDTH), BF16),
        vm((NX, BLK, COLS), BF16),
        vm((NZ, NY, NC, ROWS, BLK), BF16),
        vm((NZ, NY, ROWS, BLK), BF16),
        vm((BLK, WIDTH), BF16), vm((BLK, WIDTH), BF16),
        vm((HEADS, BLK, BLK), BF16),
        vm((BLK, WIDTH), F32),
        vm((HEADS, BLK, 1), F32),
        vm((BLK, WIDTH), F32),
        vm((BLK, WIDTH), BF16),
        vm((BLK, WIDTH), F32), vm((BLK, WIDTH), F32),
        vm((NZ, NY, ROWS, WIDTH), F32),
        vm((8, PB, WIDTH), BF16), vm((2, 8, PA, WIDTH), BF16),
        vm((2, 8, PB, WIDTH), BF16), vm((2, 8, PB, WIDTH), BF16),
        vm((8, PB, WIDTH), F32),
        vm((2, 4, PB, WIDTH), BF16), vm((2, 4, PB, WIDTH), BF16),
        vm((2, 4, NY, PA, WIDTH), BF16), vm((2, 4, NY, PA, WIDTH), BF16),
        vm((2, PA, 512), BF16), vm((2, PA, 512), BF16),
        vm((2, PA, WIDTH), BF16), vm((2, PA, WIDTH), BF16),
        vm((2, 8, HDIM, HDIM), BF16), vm((2, 8, HDIM, HDIM), BF16),
        vm((2, 8, HDIM, HDIM), F32),
        vm((2, NZ, 16, HDIM), F32), vm((2, NZ, 16, HDIM), F32),
        vm((2, NZ, 16, HDIM), F32), vm((2, NZ, 16, HDIM), F32),
        vm((2, 8, HDIM, HDIM), BF16), vm((2, 8, HDIM, HDIM), BF16),
        dma((5,)), dma((2, 2)), dma((2, 2)),
        dma((2, 2, 4)), dma((2, 2, 8)), dma((2, 2, 8)),
        dma((2, 2)), dma((2, 2)), dma((2, 2, 4)),
        dma((2, 8)), dma((2, 4)), dma((2,)),
        dma((2, 2, 8)), dma((2, 2, 8)), dma((2, 2, 4)), dma((2, 2, 4)),
        dma((2, 2)), dma((2, 2)),
        dma((2, 2, 8)), dma((2, 2, 8)), dma((2, 2, 8)), dma((2, 2, 8)),
    ]
    grad = jax.ShapeDtypeStruct((BLK, WIDTH), BF16)
    return pl.pallas_call(
        kernel,
        out_shape=(grad, grad, grad, jax.ShapeDtypeStruct((ROWS, WIDTH), F32)),
        in_specs=[pl.BlockSpec(memory_space=pl.ANY)] * 5,
        out_specs=[pl.BlockSpec(memory_space=pltpu.VMEM)] * 4,
        scratch_shapes=scratch,
        compiler_params=pltpu.CompilerParams(
            collective_id=0, has_side_effects=True, vmem_limit_bytes=56 * 1024 * 1024
        ),
        name="layer_backward",
    )(query_act, key_act, value_act, out_weight, out_cotangent)


def solution(mesh):
    finer = Mesh(mesh.devices.reshape(NZ, NY, NC, NX), ("z", "y", "c", "x"))
    spec = P(("z", "y", "c"), "x")
    return jax.shard_map(
        body, mesh=finer, in_specs=(spec,) * 5, out_specs=(spec,) * 4, check_vma=False
    )
```

```python
import functools

import jax
import jax.numpy as jnp
from jax import lax
from jax.experimental import pallas as pl
from jax.experimental.pallas import tpu as pltpu
from jax.sharding import Mesh
from jax.sharding import PartitionSpec as P

HDIM = 128
BLK = 256
EPS = 1e-06
NZ, NY, NC, NX = 8, 4, 2, 4
HEADS = 8
ROWS = 48
WIDTH = 1024
COLS = 768
SLAB = NY * NC * ROWS
PA = 16
PB = 32
F32 = jnp.float32
BF16 = jnp.bfloat16
GRADW_SCALE = 1.0 / 128.0


def dot_nn(a, b):
    return lax.dot_general(a, b, (((1,), (0,)), ((), ())), preferred_element_type=F32)


def dot_nt(a, b):
    return lax.dot_general(a, b, (((1,), (1,)), ((), ())), preferred_element_type=F32)


def dot_tn(a, b):
    return lax.dot_general(a, b, (((0,), (0,)), ((), ())), preferred_element_type=F32)


def kernel(
    q_hbm, k_hbm, v_hbm, w_hbm, cot_hbm,
    gq_hbm, gk_hbm, gv_hbm, gw_hbm,
    q, k, v, wb, cot, cot_t, cot_o, normed, scores, raw, inv, da, draw, pk, pv, gq, gk, gv, gw,
    part, st1, r1, st2, r2, red, zst, zr, qst, qr, qy1s, qy1r, qy2s, qy2r,
    own, s_send, s_recv, a_send, a_recv, a_pre, b_tot, b1_recv, b_base, b2_recv,
    c_send, c_recv, e_send, e_recv,
    load_sem, store_sem, cx1, cx2, zp_sem, yp1, yp2, qy1, qy2, zq, sib, tsib, nsib,
    ry1, ry2, rz, qz, qya, qyb, ss, sa, sb1, sb2, sc, se,
):
    z, y, c, x = (lax.axis_index(n) for n in ("z", "y", "c", "x"))
    up_z, dn_z = lax.rem(z + 1, NZ), lax.rem(z + NZ - 1, NZ)
    up_y, dn_y, far_y = lax.rem(y + 1, NY), lax.rem(y + 3, NY), lax.rem(y + 2, NY)
    up_x, dn_x, far_x = lax.rem(x + 1, NX), lax.rem(x + 3, NX), lax.rem(x + 2, NX)
    other = 1 - c
    zdir = ({"z": up_z}, {"z": dn_z})
    ydir = ({"y": up_y}, {"y": dn_y})
    xdir = ({"x": up_x}, {"x": dn_x})
    pending = []

    def send(src, dst, sems, at, device):
        copy = pltpu.make_async_remote_copy(
            src_ref=src, dst_ref=dst, send_sem=sems.at[(0, *at)], recv_sem=sems.at[(1, *at)],
            device_id=device, device_id_type=pl.DeviceIdType.MESH,
        )
        copy.start()
        pending.append(copy)
        return copy

    loads = [
        pltpu.make_async_copy(src, dst, load_sem.at[i])
        for i, (src, dst) in enumerate(
            ((cot_hbm, cot.at[x]), (w_hbm, wb.at[z, y, c]), (k_hbm, k), (v_hbm, v), (q_hbm, q))
        )
    ]
    for load in loads:
        load.start()

    peers = [{"c": other}]
    peers += [{"y": lax.rem(y + o, NY)} for o in range(1, NY)]
    peers += [{"z": lax.rem(z + o, NZ)} for o in range(1, NZ)]
    peers += list(xdir)
    barrier = pltpu.get_barrier_semaphore()
    for peer in peers:
        pl.semaphore_signal(barrier, inc=1, device_id=peer, device_id_type=pl.DeviceIdType.MESH)
    pl.semaphore_wait(barrier, len(peers))

    loads[0].wait()
    cot1 = [send(cot.at[x], cot.at[x], cx1, (d,), xdir[d]) for d in (0, 1)]
    cot2 = []

    def cot_forward():
        cot1[0].wait_recv()
        half = cot.at[dn_x, pl.ds(0, 128)]
        cot2.append(send(half, half, cx2, (0,), xdir[0]))
        cot1[1].wait_recv()
        half = cot.at[up_x, pl.ds(128, 128)]
        cot2.append(send(half, half, cx2, (1,), xdir[1]))

    ag_z = [lax.rem(z + NZ + o, NZ) for o in (0, -1, 1, -2, 2, -3, 3, 4)]
    zp_c, yp1_c, yp2_c, qy1_c, qy2_c, zq_c, sib_c = {}, {}, {}, {}, {}, {}, {}

    def send_zp(r):
        for d, org in ((0, lax.rem(z + NZ - r, NZ)), (1, lax.rem(z + r, NZ))):
            rows = pl.ds(0, PB) if r < 3 else pl.ds(PA * d, PA)
            blk = wb.at[org, y, c, rows]
            zp_c[d, r] = send(blk, blk, zp_sem, (d, r), zdir[d])

    def send_yp1(i):
        for d in (0, 1):
            blk = wb.at[ag_z[i], y, c, pl.ds(0, PB)]
            yp1_c[d, i] = send(blk, blk, yp1, (d, i), ydir[d])

    def forward_yp(i):
        for d, org in ((0, dn_y), (1, up_y)):
            yp1_c[d, i].wait_recv()
            blk = wb.at[ag_z[i], org, c, pl.ds(PA * d, PA)]
            yp2_c[d, i] = send(blk, blk, yp2, (d, i), ydir[d])

    def send_qy1():
        for d in (0, 1):
            blk = wb.at[z, y, c, pl.ds(PB, PA)]
            qy1_c[d] = send(blk, blk, qy1, (d,), ydir[d])

    def forward_qy():
        for d, org in ((0, dn_y), (1, up_y)):
            qy1_c[d].wait_recv()
            blk = wb.at[z, org, c, pl.ds(PB, PA), pl.ds(512 * d, 512)]
            qy2_c[d] = send(blk, blk, qy2, (d,), ydir[d])

    q_rows = (y, dn_y, up_y, far_y)

    def send_zq(b, r):
        if r > 0:
            for d in (0, 1):
                zq_c[b, d, r - 1].wait_recv()
        for d, org in ((0, lax.rem(z + NZ - r, NZ)), (1, lax.rem(z + r, NZ))):
            lanes = pl.ds(0, WIDTH) if r < 3 else pl.ds(512 * d, 512)
            blk = wb.at[org, q_rows[b], c, pl.ds(PB, PA), lanes]
            zq_c[b, d, r] = send(blk, blk, zq, (b, d, r), zdir[d])

    def recv_both(copies, r):
        for d in (0, 1):
            copies[d, r].wait_recv()

    def ag_start():
        send_zp(0)
        send_qy1()
        send_zq(0, 0)
        send_yp1(0)

    def ag_q1():
        forward_qy()
        send_zq(1, 0)
        send_zq(2, 0)

    def ag_q2():
        qy2_c[0].wait_recv()
        qy2_c[1].wait_recv()
        send_zq(3, 0)

    def ag_p(r):
        recv_both(zp_c, r - 1)
        if r < 4:
            send_zp(r)
            send_yp1(2 * r - 1)
            send_yp1(2 * r)
        else:
            send_yp1(7)

    def send_sib(i):
        recv_both(yp2_c, i)
        if i == 7:
            for b in range(4):
                zq_c[b, 0, 3].wait_recv()
                zq_c[b, 1, 3].wait_recv()
        blk = wb.at[ag_z[i], :, c]
        sib_c[i] = send(blk, blk, sib, (i,), {"c": other})

    order = (range(8), range(7, -1, -1))
    y_order = (range(NY), range(NY - 1, -1, -1))
    s_c, a_c, b1_c, b2_c, c_c, e_c = {}, {}, {}, {}, {}, {}
    mine4, rest4 = pl.ds(c * 4, 4), pl.ds(other * 4, 4)

    def scan_start(s):
        s_send[s] = own[s, rest4].astype(BF16)
        s_c[s] = send(s_send.at[s], s_recv.at[s], ss, (s,), {"c": other})

    def scan_a(s):
        s_c[s].wait_recv()
        total = own[s, mine4] + s_recv[s].astype(F32)
        a_send[s] = total.astype(BF16)
        for o in range(1, NY):
            t = lax.rem(y + o, NY)
            a_c[s, o] = send(a_send.at[s, t], a_recv.at[s, y], sa, (s, o), {"y": t})
        a_recv[s, y] = a_send[s, y]

    def scan_b1(s):
        for o in range(1, NY):
            a_c[s, o].wait_recv()
        run = jnp.zeros((HDIM, HDIM), F32)
        for t in y_order[s]:
            a_pre[s, t] = run
            run = run + a_recv[s, t].astype(F32)
        b_tot[s] = run.reshape(NZ, 16, HDIM)
        for o in range(1, NZ):
            t = lax.rem(z + o, NZ)
            b1_c[s, o] = send(b_tot.at[s, t], b1_recv.at[s, z], sb1, (s, o), {"z": t})
        b1_recv[s, z] = b_tot[s, z]

    def scan_b2(s):
        for o in range(1, NZ):
            b1_c[s, o].wait_recv()
        run = jnp.zeros((16, HDIM), F32)
        for t in order[s]:
            b_base[s, t] = run
            run = run + b1_recv[s, t]
        for o in range(1, NZ):
            t = lax.rem(z + o, NZ)
            b2_c[s, o] = send(b_base.at[s, t], b2_recv.at[s, z], sb2, (s, o), {"z": t})
        b2_recv[s, z] = b_base[s, z]

    def scan_c(s):
        for o in range(1, NZ):
            b2_c[s, o].wait_recv()
        base = b2_recv[s].reshape(HDIM, HDIM)
        for t in range(NY):
            c_send[s, t] = (base + a_pre[s, t]).astype(BF16)
        for o in range(1, NY):
            t = lax.rem(y + o, NY)
            c_c[s, o] = send(c_send.at[s, t], c_recv.at[s, y], sc, (s, o), {"y": t})
        c_recv[s, y] = c_send[s, y]

    def scan_e(s):
        for o in range(1, NY):
            c_c[s, o].wait_recv()
        first = c == s
        outer = c_recv[s].astype(F32)
        after_own = outer + own[s, mine4]
        after_sib = outer + s_recv[s].astype(F32)
        e_send[s] = jnp.where(first, after_own, outer).astype(BF16)
        e_c[s] = send(e_send.at[s], e_recv.at[s, mine4], se, (s,), {"c": other})
        e_recv[s, mine4] = jnp.where(first, outer, after_sib).astype(BF16)

    def scan_end(s):
        e_c[s].wait_recv()

    def cols_of(h):
        return pl.ds(pl.multiple_of(h * HDIM, HDIM), HDIM)

    def for_heads(first, count, fn, unroll=2):
        @pl.loop(0, count // unroll)
        def _(i):
            for u in range(unroll):
                fn(first + i * unroll + u)

    mask = (
        lax.broadcasted_iota(jnp.int32, (BLK, BLK), 0)
        >= lax.broadcasted_iota(jnp.int32, (BLK, BLK), 1)
    )

    def kv_head(h):
        cs = cols_of(h)
        own[0, h] = dot_tn(k[:, cs], v[:, cs])

    def score_head(h):
        cs = cols_of(h)
        s = jnp.where(mask, dot_nt(q[:, cs], k[:, cs]), 0.0).astype(BF16)
        scores[h] = s
        raw[:, cs] = dot_nn(s, v[:, cs])

    def norm_head(h):
        cs = cols_of(h)
        r = raw[:, cs] + dot_nn(q[:, cs], e_recv[0, h])
        i = lax.rsqrt(jnp.mean(r * r, axis=-1, keepdims=True) + EPS)
        a = r * i
        raw[:, cs] = a
        inv[h] = i
        normed[0:BLK, cs] = a.astype(BF16)

    def draw_head(h):
        cs = cols_of(h)
        d, a = da[:, cs], raw[:, cs]
        center = jnp.mean(d * a, axis=-1, keepdims=True)
        dr = (inv[h] * (d - a * center)).astype(BF16)
        draw[:, cs] = dr
        own[1, h] = dot_tn(q[:, cs], dr)

    def local_grad_head(h):
        cs = cols_of(h)
        dr = draw[:, cs]
        ds = jnp.where(mask, dot_nt(dr, v[:, cs]), 0.0).astype(BF16)
        gq[:, cs] = (dot_nn(ds, k[:, cs]) + dot_nt(dr, e_recv[0, h])).astype(BF16)
        pk[:, cs] = dot_tn(ds, q[:, cs])
        pv[:, cs] = dot_tn(scores[h], dr)

    def final_grad_head(h):
        cs = cols_of(h)
        gk[:, cs] = (pk[:, cs] + dot_nt(v[:, cs], e_recv[1, h])).astype(BF16)
        gv[:, cs] = (pv[:, cs] + dot_nn(k[:, cs], e_recv[1, h])).astype(BF16)

    x_order = (x, dn_x, up_x, far_x)
    tsib_c = {}

    def turn(i):
        xo = x_order[i]
        for half in (0, 1):
            far_first = lax.rem(xo * 2 + half - z + NZ, NZ)
            zi = jnp.where(far_first < 4, 7 - 2 * far_first, 2 * far_first - 8)
            t = cot[xo, :, pl.ds(half * SLAB, SLAB)].T.reshape(NY, NC, ROWS, BLK)
            for yt in range(NY):
                dy = lax.rem(yt - y + NY, NY)
                yi = jnp.where(dy == 0, 3, jnp.where(dy == 2, 0, jnp.where(dy == 1, 1, 2)))
                keep = jnp.where(c == 0, t[yt, 0], t[yt, 1])
                give = jnp.where(c == 0, t[yt, 1], t[yt, 0])
                cot_t[zi, yi, :, 0:BLK] = keep
                cot_o[zi, yi] = give
            tsib_c[i, half] = send(
                cot_o.at[zi], cot_t.at[zi, :, :, pl.ds(BLK, BLK)], tsib, (i, half), {"c": other}
            )

    def d_attn(idx, first=False):
        for i in idx:
            sib_c[i].wait_recv()

        @pl.loop(0, 4)
        def _(n):
            cs = pl.ds(pl.multiple_of(n * 256, 256), 256)
            lhs, rhs = [], []
            for i in idx:
                zo = ag_z[i]
                lanes = pl.ds(pl.multiple_of(lax.rem(zo, 2) * SLAB, 128), SLAB)
                lhs.append(cot[lax.div(zo, 2), :, lanes])
                rhs.append(wb[zo, :, :, :, cs].reshape(SLAB, 256))
            t = dot_nn(jnp.concatenate(lhs, 1), jnp.concatenate(rhs, 0))
            da[:, cs] = t if first else da[:, cs] + t

    up_of, dn_of = (0, 1, 3, 5), (0, 2, 4, 6)
    y_of = (1, 2)
    ry1_c, ry2_c, rz_c, qz_c, qya_c, qyb_c = {}, {}, {}, {}, {}, {}

    def product(lo, hi):
        n = hi - lo

        @pl.loop(0, 4)
        def _(col):
            cs = pl.ds(pl.multiple_of(col * 256, 256), 256)
            acc = dot_nn(cot_t[lo:hi].reshape(n * NY * ROWS, 2 * BLK), normed[:, cs])
            part[lo:hi, :, :, cs] = acc.reshape(n, NY, ROWS, 256)

    def step1(i):
        st1[i] = part[i, 0, 0:PB].astype(BF16)
        for d in (0, 1):
            ry1_c[d, i] = send(st1.at[i, pl.ds(PA * d, PA)], r1.at[d, i], ry1, (d, i), ydir[d])

    def step2(i):
        for d in (0, 1):
            t = y_of[d]
            ry1_c[d, i].wait_recv()
            mine, rest = slice(PA * d, PA * d + PA), slice(PA - PA * d, PB - PA * d)
            st2[d, i, mine] = (part[i, t, mine] + r1[d, i].astype(F32)).astype(BF16)
            st2[d, i, rest] = part[i, t, rest].astype(BF16)
            ry2_c[d, i] = send(st2.at[d, i], r2.at[d, i], ry2, (d, i), ydir[d])

    def step3(i):
        recv_both(ry2_c, i)
        red[i] = part[i, 3, 0:PB] + (r2[0, i].astype(F32) + r2[1, i].astype(F32))

    def chain(s):
        for d, idx in ((0, up_of), (1, dn_of)):
            i = idx[s]
            mine = slice(PA * d, PA * d + PA)
            if s == 0:
                zst[d, 0, mine] = red[i, mine].astype(BF16)
                blk = pl.ds(PA * d, PA)
                rz_c[d, s] = send(zst.at[d, 0, blk], zr.at[d, 0, blk], rz, (d, s), zdir[d])
                continue
            rz_c[d, s - 1].wait_recv()
            if s == 1:
                rest = slice(PA - PA * d, PB - PA * d)
                zst[d, s, mine] = (red[i, mine] + zr[d, 0, mine].astype(F32)).astype(BF16)
                zst[d, s, rest] = red[i, rest].astype(BF16)
            else:
                zst[d, s] = (red[i] + zr[d, s - 1].astype(F32)).astype(BF16)
            rz_c[d, s] = send(zst.at[d, s], zr.at[d, s], rz, (d, s), zdir[d])

    def chain_end():
        recv_both(rz_c, 3)
        total = red[7] + (zr[0, 3].astype(F32) + zr[1, 3].astype(F32))
        gw[0:PB] = total * GRADW_SCALE

    def qchain(b, s):
        ys = pl.ds(2 * b, 2)
        for d, idx in ((0, up_of), (1, dn_of)):
            i = idx[s]
            term = part[i, 2 * b : 2 * b + 2, PB:ROWS]
            if s > 0:
                qz_c[b, d, s - 1].wait_recv()
            if s == 0:
                t = 2 * b + d
                qst[d, 0, t] = part[i, t, PB:ROWS].astype(BF16)
                blk = pl.ds(t, 1)
                qz_c[b, d, s] = send(qst.at[d, 0, blk], qr.at[d, 0, blk], qz, (b, d, s), zdir[d])
                continue
            if s == 1:
                t, u = 2 * b + d, 2 * b + 1 - d
                qst[d, s, t] = (part[i, t, PB:ROWS] + qr[d, 0, t].astype(F32)).astype(BF16)
                qst[d, s, u] = part[i, u, PB:ROWS].astype(BF16)
            else:
                got = qr[d, s - 1, 2 * b : 2 * b + 2].astype(F32)
                qst[d, s, 2 * b : 2 * b + 2] = (term + got).astype(BF16)
            qz_c[b, d, s] = send(qst.at[d, s, ys], qr.at[d, s, ys], qz, (b, d, s), zdir[d])

    def q_sum(b):
        for d in (0, 1):
            qz_c[b, d, 3].wait_recv()
        ys = slice(2 * b, 2 * b + 2)
        got = qr[0, 3, ys].astype(F32) + qr[1, 3, ys].astype(F32)
        part[7, ys, PB:ROWS] = part[7, ys, PB:ROWS] + got

    def q_y1():
        q_sum(0)
        for d in (0, 1):
            qy1s[d] = part[7, 0, PB:ROWS, 512 * d : 512 * d + 512].astype(BF16)
            qya_c[d] = send(qy1s.at[d], qy1r.at[d], qya, (d,), ydir[d])

    def q_y2():
        q_sum(1)
        for d in (0, 1):
            t = y_of[d]
            qya_c[d].wait_recv()
            mine = slice(512 * d, 512 * d + 512)
            rest = slice(512 - 512 * d, 1024 - 512 * d)
            qy2s[d, :, mine] = (part[7, t, PB:ROWS, mine] + qy1r[d].astype(F32)).astype(BF16)
            qy2s[d, :, rest] = part[7, t, PB:ROWS, rest].astype(BF16)
            qyb_c[d] = send(qy2s.at[d], qy2r.at[d], qyb, (d,), ydir[d])

    def q_end():
        for d in (0, 1):
            qyb_c[d].wait_recv()
        total = part[7, 3, PB:ROWS] + (qy2r[0].astype(F32) + qy2r[1].astype(F32))
        gw[PB:ROWS] = total * GRADW_SCALE

    stores = []

    def store(i, src_ref, dst_ref):
        copy = pltpu.make_async_copy(src_ref, dst_ref, store_sem.at[i])
        copy.start()
        stores.append(copy)

    half8 = ((0, 4), (4, 4))
    nsib_c = []

    def kv():
        loads[2].wait()
        loads[3].wait()
        for_heads(0, 8, kv_head, 4)

    def score(n):
        if n == 0:
            loads[4].wait()
        for_heads(*half8[n], score_head, 4)

    def norm(n):
        for_heads(*half8[n], norm_head, 4)
        blk = pl.ds(512 * n, 512)
        src, dst = normed.at[pl.ds(0, BLK), blk], normed.at[pl.ds(BLK, BLK), blk]
        nsib_c.append(send(src, dst, nsib, (n,), {"c": other}))

    def cot_wait():
        for copy in cot2:
            copy.wait_recv()

    def sib_wait():
        for copy in nsib_c:
            copy.wait_recv()
        for copy in tsib_c.values():
            copy.wait_recv()

    def local_grad(n):
        for_heads(*half8[n], local_grad_head, 4)
        if n == 1:
            store(0, gq, gq_hbm)

    def final_grad():
        for_heads(0, 8, final_grad_head, 4)
        store(1, gk, gk_hbm)
        store(2, gv, gv_hbm)

    loads[1].wait()
    ag_start()
    kv()
    scan_start(0)
    score(0)
    score(1)
    scan_a(0)
    ag_q1()
    forward_yp(0)
    ag_p(1)
    send_zq(0, 1)
    turn(0)
    send_zq(1, 1)
    ag_q2()
    send_zq(2, 1)
    scan_b1(0)
    send_sib(0)
    ag_p(2)
    cot_forward()
    forward_yp(1)
    send_zq(0, 2)
    turn(1)
    forward_yp(2)
    send_zq(1, 2)
    send_zq(3, 1)
    turn(2)
    send_zq(2, 2)
    forward_yp(3)
    scan_b2(0)
    forward_yp(4)
    ag_p(3)
    send_zq(0, 3)
    send_sib(1)
    send_sib(2)
    send_zq(1, 3)
    cot_wait()
    turn(3)
    send_zq(3, 2)
    send_zq(2, 3)
    send_sib(3)
    send_sib(4)
    d_attn((0, 1, 2), True)
    scan_c(0)
    forward_yp(5)
    forward_yp(6)
    ag_p(4)
    send_zq(3, 3)
    d_attn((3, 4))
    send_sib(5)
    scan_e(0)
    send_sib(6)
    forward_yp(7)
    scan_end(0)
    norm(0)
    norm(1)
    d_attn((5, 6))
    send_sib(7)
    sib_wait()
    product(0, 1)
    qchain(0, 0)
    qchain(1, 0)
    step1(0)
    product(1, 3)
    d_attn((7,))
    for_heads(0, 8, draw_head, 4)
    scan_start(1)
    qchain(0, 1)
    qchain(1, 1)
    step2(0)
    step1(1)
    step1(2)
    scan_a(1)
    product(3, 5)
    step1(3)
    step1(4)
    product(5, 8)
    step3(0)
    chain(0)
    qchain(0, 2)
    qchain(1, 2)
    step2(1)
    step2(2)
    step1(5)
    step1(6)
    step1(7)
    local_grad(0)
    scan_b1(1)
    step2(3)
    step2(4)
    qchain(0, 3)
    step3(1)
    local_grad(1)
    step3(2)
    chain(1)
    qchain(1, 3)
    step2(5)
    step2(6)
    step2(7)
    scan_b2(1)
    q_y1()
    step3(3)
    step3(4)
    chain(2)
    step3(5)
    step3(6)
    scan_c(1)
    chain(3)
    step3(7)
    q_y2()
    chain_end()
    q_end()
    scan_e(1)
    scan_end(1)
    final_grad()
    store(3, gw, gw_hbm)
    for copy in stores:
        copy.wait()
    for copy in pending:
        copy.wait_send()


def handed_out(*refs):
    ins, outs, held, sems = refs[:4], refs[4:8], refs[8:12], refs[12]
    into = [pltpu.make_async_copy(a, b, sems.at[0, i]) for i, (a, b) in enumerate(zip(ins, held))]
    back = [pltpu.make_async_copy(a, b, sems.at[1, i]) for i, (a, b) in enumerate(zip(held, outs))]
    for copy in into:
        copy.start()
    for i in range(4):
        into[i].wait()
        back[i].start()
    for copy in back:
        copy.wait()


def body(query_act, key_act, value_act, out_weight, out_cotangent):
    vm = pltpu.VMEM
    dma = pltpu.SemaphoreType.DMA
    state = (HDIM, HDIM)
    scratch = [
        vm((BLK, WIDTH), BF16), vm((BLK, WIDTH), BF16), vm((BLK, WIDTH), BF16),
        vm((NZ, NY, NC, ROWS, WIDTH), BF16),
        vm((NX, BLK, COLS), BF16),
        vm((NZ, NY, ROWS, 2 * BLK), BF16), vm((NZ, NY, ROWS, BLK), BF16),
        vm((2 * BLK, WIDTH), BF16),
        vm((HEADS, BLK, BLK), BF16),
        vm((BLK, WIDTH), F32),
        vm((HEADS, BLK, 1), F32),
        vm((BLK, WIDTH), F32),
        vm((BLK, WIDTH), BF16),
        vm((BLK, WIDTH), F32), vm((BLK, WIDTH), F32),
        vm((BLK, WIDTH), BF16), vm((BLK, WIDTH), BF16), vm((BLK, WIDTH), BF16),
        vm((ROWS, WIDTH), F32),
        vm((NZ, NY, ROWS, WIDTH), F32),
        vm((8, PB, WIDTH), BF16), vm((2, 8, PA, WIDTH), BF16),
        vm((2, 8, PB, WIDTH), BF16), vm((2, 8, PB, WIDTH), BF16),
        vm((8, PB, WIDTH), F32),
        vm((2, 4, PB, WIDTH), BF16), vm((2, 4, PB, WIDTH), BF16),
        vm((2, 4, NY, PA, WIDTH), BF16), vm((2, 4, NY, PA, WIDTH), BF16),
        vm((2, PA, 512), BF16), vm((2, PA, 512), BF16),
        vm((2, PA, WIDTH), BF16), vm((2, PA, WIDTH), BF16),
        vm((2, HEADS, *state), F32),
        vm((2, 4, *state), BF16), vm((2, 4, *state), BF16),
        vm((2, 4, *state), BF16), vm((2, 4, *state), BF16), vm((2, 4, *state), F32),
        vm((2, NZ, 16, HDIM), F32), vm((2, NZ, 16, HDIM), F32),
        vm((2, NZ, 16, HDIM), F32), vm((2, NZ, 16, HDIM), F32),
        vm((2, 4, *state), BF16), vm((2, 4, *state), BF16),
        vm((2, 4, *state), BF16), vm((2, HEADS, *state), BF16),
        dma((5,)), dma((4,)), dma((2, 2)), dma((2, 2)),
        dma((2, 2, 4)), dma((2, 2, 8)), dma((2, 2, 8)),
        dma((2, 2)), dma((2, 2)), dma((2, 4, 2, 4)),
        dma((2, 8)), dma((2, 4, 2)), dma((2, 2)),
        dma((2, 2, 8)), dma((2, 2, 8)), dma((2, 2, 4)), dma((2, 2, 2, 4)),
        dma((2, 2)), dma((2, 2)),
        dma((2, 2)), dma((2, 2, 4)), dma((2, 2, 8)), dma((2, 2, 8)), dma((2, 2, 4)), dma((2, 2)),
    ]
    grad = jax.ShapeDtypeStruct((BLK, WIDTH), BF16)
    shapes = (grad, grad, grad, jax.ShapeDtypeStruct((ROWS, WIDTH), F32))
    anywhere = pl.BlockSpec(memory_space=pl.ANY)
    made = pl.pallas_call(
        kernel,
        out_shape=shapes,
        in_specs=[anywhere] * 5,
        out_specs=[anywhere] * 4,
        scratch_shapes=scratch,
        compiler_params=pltpu.CompilerParams(
            collective_id=0, has_side_effects=True, vmem_limit_bytes=56 * 1024 * 1024
        ),
        name="layer_backward",
    )(query_act, key_act, value_act, out_weight, out_cotangent)
    return pl.pallas_call(
        handed_out,
        out_shape=shapes,
        in_specs=[anywhere] * 4,
        out_specs=[anywhere] * 4,
        scratch_shapes=[*(vm(s.shape, s.dtype) for s in shapes), dma((2, 4))],
        name="hand_out",
    )(*made)


def solution(mesh):
    finer = Mesh(mesh.devices.reshape(NZ, NY, NC, NX), ("z", "y", "c", "x"))
    spec = P(("z", "y", "c"), "x")
    return jax.shard_map(
        body, mesh=finer, in_specs=(spec,) * 5, out_specs=(spec,) * 4, check_vma=False
    )
```

```python
import functools

import jax
import jax.numpy as jnp
from jax import lax
from jax.experimental import pallas as pl
from jax.experimental.pallas import tpu as pltpu
from jax.sharding import Mesh
from jax.sharding import PartitionSpec as P

HDIM = 128
BLK = 256
EPS = 1e-06
NZ, NY, NC, NX = 8, 4, 2, 4
CHIPS = NZ * NY
HEADS = 8
ROWS = 48
WIDTH = 1024
COLS = 768
SLAB = NY * NC * ROWS
PA = 16
PB = 32
F32 = jnp.float32
BF16 = jnp.bfloat16
GRADW_SCALE = 1.0 / 128.0


def dot_nn(a, b):
    return lax.dot_general(a, b, (((1,), (0,)), ((), ())), preferred_element_type=F32)


def dot_nt(a, b):
    return lax.dot_general(a, b, (((1,), (1,)), ((), ())), preferred_element_type=F32)


def dot_tn(a, b):
    return lax.dot_general(a, b, (((0,), (0,)), ((), ())), preferred_element_type=F32)


def kernel(
    q_hbm, k_hbm, v_hbm, w_hbm, cot_hbm,
    gq_hbm, gk_hbm, gv_hbm, gw_hbm,
    q, k, v, wb, cot, cot_t, cot_o, normed, scores, raw, inv, da, draw, pk, pv, gq, gk, gv, gw,
    part, st1, r1, st2, r2, red, zst, zr, qst, qr, qy1s, qy1r, qy2s, qy2r,
    own, s_send, s_recv, a_send, a_recv, c_send, c_recv, e_send, e_recv,
    load_sem, store_sem, cx1, cx2, zp_sem, yp1, yp2, qy1, qy2, zq, sib, tsib, nsib,
    ry1, ry2, rz, qz, qya, qyb, ss, sa, sc, se,
):
    z, y, c, x = (lax.axis_index(n) for n in ("z", "y", "c", "x"))
    up_z, dn_z = lax.rem(z + 1, NZ), lax.rem(z + NZ - 1, NZ)
    up_y, dn_y, far_y = lax.rem(y + 1, NY), lax.rem(y + 3, NY), lax.rem(y + 2, NY)
    up_x, dn_x, far_x = lax.rem(x + 1, NX), lax.rem(x + 3, NX), lax.rem(x + 2, NX)
    other = 1 - c
    zdir = ({"z": up_z}, {"z": dn_z})
    ydir = ({"y": up_y}, {"y": dn_y})
    xdir = ({"x": up_x}, {"x": dn_x})
    pending = []

    def send(src, dst, sems, at, device):
        copy = pltpu.make_async_remote_copy(
            src_ref=src, dst_ref=dst, send_sem=sems.at[(0, *at)], recv_sem=sems.at[(1, *at)],
            device_id=device, device_id_type=pl.DeviceIdType.MESH,
        )
        copy.start()
        pending.append(copy)
        return copy

    loads = [
        pltpu.make_async_copy(src, dst, load_sem.at[i])
        for i, (src, dst) in enumerate(
            ((cot_hbm, cot.at[x]), (w_hbm, wb.at[z, y, c]), (k_hbm, k), (v_hbm, v), (q_hbm, q))
        )
    ]
    for load in loads:
        load.start()

    chip = z * NY + y

    def chip_peer(o):
        t = lax.rem(chip + o, CHIPS)
        return t, {"z": lax.div(t, NY), "y": lax.rem(t, NY)}

    barrier = pltpu.get_barrier_semaphore()

    def greet(peer):
        pl.semaphore_signal(barrier, inc=1, device_id=peer, device_id_type=pl.DeviceIdType.MESH)

    @pl.loop(1, CHIPS)
    def _(o):
        greet(chip_peer(o)[1])

    for peer in ({"c": other}, *xdir):
        greet(peer)

    def cols_of(h):
        return pl.ds(pl.multiple_of(h * HDIM, HDIM), HDIM)

    def for_heads(first, count, fn, unroll=2):
        @pl.loop(0, count // unroll)
        def _(i):
            for u in range(unroll):
                fn(first + i * unroll + u)

    mask = (
        lax.broadcasted_iota(jnp.int32, (BLK, BLK), 0)
        >= lax.broadcasted_iota(jnp.int32, (BLK, BLK), 1)
    )

    def kv_head(h):
        cs = cols_of(h)
        own[0, h] = dot_tn(k[:, cs], v[:, cs])

    def score_head(h):
        cs = cols_of(h)
        s = jnp.where(mask, dot_nt(q[:, cs], k[:, cs]), 0.0).astype(BF16)
        scores[h] = s
        raw[:, cs] = dot_nn(s, v[:, cs])

    def norm_head(h):
        cs = cols_of(h)
        r = raw[:, cs] + dot_nn(q[:, cs], e_recv[0, h])
        i = lax.rsqrt(jnp.mean(r * r, axis=-1, keepdims=True) + EPS)
        a = r * i
        raw[:, cs] = a
        inv[h] = i
        normed[0:BLK, cs] = a.astype(BF16)

    def draw_head(h):
        cs = cols_of(h)
        d, a = da[:, cs], raw[:, cs]
        center = jnp.mean(d * a, axis=-1, keepdims=True)
        dr = (inv[h] * (d - a * center)).astype(BF16)
        draw[:, cs] = dr
        own[1, h] = dot_tn(q[:, cs], dr)

    def local_grad_head(h):
        cs = cols_of(h)
        dr = draw[:, cs]
        ds = jnp.where(mask, dot_nt(dr, v[:, cs]), 0.0).astype(BF16)
        gq[:, cs] = (dot_nn(ds, k[:, cs]) + dot_nt(dr, e_recv[0, h])).astype(BF16)
        pk[:, cs] = dot_tn(ds, q[:, cs])
        pv[:, cs] = dot_tn(scores[h], dr)

    def final_grad_head(h):
        cs = cols_of(h)
        gk[:, cs] = (pk[:, cs] + dot_nt(v[:, cs], e_recv[1, h])).astype(BF16)
        gv[:, cs] = (pv[:, cs] + dot_nn(k[:, cs], e_recv[1, h])).astype(BF16)

    for i in (2, 3):
        loads[i].wait()
    for_heads(0, 8, kv_head, 4)
    loads[4].wait()
    for_heads(0, 8, score_head, 4)
    pl.semaphore_wait(barrier, CHIPS + 2)

    loads[0].wait()
    cot1 = [send(cot.at[x], cot.at[x], cx1, (d,), xdir[d]) for d in (0, 1)]
    cot2 = []

    def cot_forward():
        cot1[0].wait_recv()
        half = cot.at[dn_x, pl.ds(0, 128)]
        cot2.append(send(half, half, cx2, (0,), xdir[0]))
        cot1[1].wait_recv()
        half = cot.at[up_x, pl.ds(128, 128)]
        cot2.append(send(half, half, cx2, (1,), xdir[1]))

    ag_z = [lax.rem(z + NZ + o, NZ) for o in (0, -1, 1, -2, 2, -3, 3, 4)]
    zp_c, yp1_c, yp2_c, qy1_c, qy2_c, zq_c, sib_c = {}, {}, {}, {}, {}, {}, {}

    def send_zp(r):
        for d, org in ((0, lax.rem(z + NZ - r, NZ)), (1, lax.rem(z + r, NZ))):
            rows = pl.ds(0, PB) if r < 3 else pl.ds(PA * d, PA)
            blk = wb.at[org, y, c, rows]
            zp_c[d, r] = send(blk, blk, zp_sem, (d, r), zdir[d])

    def send_yp1(i):
        for d in (0, 1):
            blk = wb.at[ag_z[i], y, c, pl.ds(0, PB)]
            yp1_c[d, i] = send(blk, blk, yp1, (d, i), ydir[d])

    def forward_yp(i):
        for d, org in ((0, dn_y), (1, up_y)):
            yp1_c[d, i].wait_recv()
            blk = wb.at[ag_z[i], org, c, pl.ds(PA * d, PA)]
            yp2_c[d, i] = send(blk, blk, yp2, (d, i), ydir[d])

    def send_qy1():
        for d in (0, 1):
            blk = wb.at[z, y, c, pl.ds(PB, PA)]
            qy1_c[d] = send(blk, blk, qy1, (d,), ydir[d])

    def forward_qy():
        for d, org in ((0, dn_y), (1, up_y)):
            qy1_c[d].wait_recv()
            blk = wb.at[z, org, c, pl.ds(PB, PA), pl.ds(512 * d, 512)]
            qy2_c[d] = send(blk, blk, qy2, (d,), ydir[d])

    q_rows = (y, dn_y, up_y, far_y)

    def send_zq(b, r):
        if r > 0:
            for d in (0, 1):
                zq_c[b, d, r - 1].wait_recv()
        for d, org in ((0, lax.rem(z + NZ - r, NZ)), (1, lax.rem(z + r, NZ))):
            lanes = pl.ds(0, WIDTH) if r < 3 else pl.ds(512 * d, 512)
            blk = wb.at[org, q_rows[b], c, pl.ds(PB, PA), lanes]
            zq_c[b, d, r] = send(blk, blk, zq, (b, d, r), zdir[d])

    def recv_both(copies, r):
        for d in (0, 1):
            copies[d, r].wait_recv()

    def ag_start():
        send_zp(0)
        send_qy1()
        send_zq(0, 0)
        send_yp1(0)

    def ag_q1():
        forward_qy()
        send_zq(1, 0)
        send_zq(2, 0)

    def ag_q2():
        qy2_c[0].wait_recv()
        qy2_c[1].wait_recv()
        send_zq(3, 0)

    def ag_p(r):
        recv_both(zp_c, r - 1)
        if r < 4:
            send_zp(r)
            send_yp1(2 * r - 1)
            send_yp1(2 * r)
        else:
            send_yp1(7)

    def send_sib(i):
        recv_both(yp2_c, i)
        if i == 7:
            for b in range(4):
                zq_c[b, 0, 3].wait_recv()
                zq_c[b, 1, 3].wait_recv()
        blk = wb.at[ag_z[i], :, c]
        sib_c[i] = send(blk, blk, sib, (i,), {"c": other})

    order = (range(CHIPS), range(CHIPS - 1, -1, -1))
    s_c, e_c = {}, {}
    mine4, rest4 = pl.ds(c * 4, 4), pl.ds(other * 4, 4)
    state4 = (4, HDIM, HDIM)

    def spread(src, dst, sem, s):
        @pl.loop(1, CHIPS)
        def _(o):
            t, dev = chip_peer(o)
            pltpu.make_async_remote_copy(
                src_ref=src.at[s, t], dst_ref=dst.at[s, chip],
                send_sem=sem.at[0, s], recv_sem=sem.at[1, s],
                device_id=dev, device_id_type=pl.DeviceIdType.MESH,
            ).start()

        dst[s, chip] = src[s, chip]
        all_but_one = pl.ds(0, CHIPS - 1)
        whole = pltpu.make_async_remote_copy(
            src_ref=src.at[s, all_but_one], dst_ref=dst.at[s, all_but_one],
            send_sem=sem.at[0, s], recv_sem=sem.at[1, s],
            device_id=chip_peer(1)[1], device_id_type=pl.DeviceIdType.MESH,
        )
        pending.append(whole)
        return whole

    a_c, c_c = {}, {}

    def scan_start(s):
        s_send[s] = own[s, rest4].astype(BF16)
        s_c[s] = send(s_send.at[s], s_recv.at[s], ss, (s,), {"c": other})

    def scan_a(s):
        s_c[s].wait_recv()
        total = own[s, mine4] + s_recv[s].astype(F32)
        a_send[s] = total.astype(BF16).reshape(CHIPS, 16, HDIM)
        a_c[s] = spread(a_send, a_recv, sa, s)

    def scan_c(s):
        a_c[s].wait_recv()
        run = jnp.zeros((16, HDIM), F32)
        for t in order[s]:
            c_send[s, t] = run.astype(BF16)
            run = run + a_recv[s, t].astype(F32)
        c_c[s] = spread(c_send, c_recv, sc, s)

    def scan_e(s):
        c_c[s].wait_recv()
        first = c == s
        outer = c_recv[s].reshape(state4).astype(F32)
        after_own = outer + own[s, mine4]
        after_sib = outer + s_recv[s].astype(F32)
        e_send[s] = jnp.where(first, after_own, outer).astype(BF16)
        e_c[s] = send(e_send.at[s], e_recv.at[s, mine4], se, (s,), {"c": other})
        e_recv[s, mine4] = jnp.where(first, outer, after_sib).astype(BF16)

    def scan_end(s):
        e_c[s].wait_recv()

    x_order = (x, dn_x, up_x, far_x)
    tsib_c = {}

    def turn(i):
        xo = x_order[i]
        for half in (0, 1):
            far_first = lax.rem(xo * 2 + half - z + NZ, NZ)
            zi = jnp.where(far_first < 4, 7 - 2 * far_first, 2 * far_first - 8)
            t = cot[xo, :, pl.ds(half * SLAB, SLAB)].T.reshape(NY, NC, ROWS, BLK)
            for yt in range(NY):
                dy = lax.rem(yt - y + NY, NY)
                yi = jnp.where(dy == 0, 3, jnp.where(dy == 2, 0, jnp.where(dy == 1, 1, 2)))
                keep = jnp.where(c == 0, t[yt, 0], t[yt, 1])
                give = jnp.where(c == 0, t[yt, 1], t[yt, 0])
                cot_t[zi, yi, :, 0:BLK] = keep
                cot_o[zi, yi] = give
            tsib_c[i, half] = send(
                cot_o.at[zi], cot_t.at[zi, :, :, pl.ds(BLK, BLK)], tsib, (i, half), {"c": other}
            )

    def d_attn(idx, first=False):
        for i in idx:
            sib_c[i].wait_recv()

        @pl.loop(0, 4)
        def _(n):
            cs = pl.ds(pl.multiple_of(n * 256, 256), 256)
            lhs, rhs = [], []
            for i in idx:
                zo = ag_z[i]
                lanes = pl.ds(pl.multiple_of(lax.rem(zo, 2) * SLAB, 128), SLAB)
                lhs.append(cot[lax.div(zo, 2), :, lanes])
                rhs.append(wb[zo, :, :, :, cs].reshape(SLAB, 256))
            t = dot_nn(jnp.concatenate(lhs, 1), jnp.concatenate(rhs, 0))
            da[:, cs] = t if first else da[:, cs] + t

    up_of, dn_of = (0, 1, 3, 5), (0, 2, 4, 6)
    y_of = (1, 2)
    ry1_c, ry2_c, rz_c, qz_c, qya_c, qyb_c = {}, {}, {}, {}, {}, {}

    def product(lo, hi):
        n = hi - lo

        @pl.loop(0, 4)
        def _(col):
            cs = pl.ds(pl.multiple_of(col * 256, 256), 256)
            acc = dot_nn(cot_t[lo:hi].reshape(n * NY * ROWS, 2 * BLK), normed[:, cs])
            part[lo:hi, :, :, cs] = acc.reshape(n, NY, ROWS, 256)

    def step1(i):
        st1[i] = part[i, 0, 0:PB].astype(BF16)
        for d in (0, 1):
            ry1_c[d, i] = send(st1.at[i, pl.ds(PA * d, PA)], r1.at[d, i], ry1, (d, i), ydir[d])

    def step2(i):
        for d in (0, 1):
            t = y_of[d]
            ry1_c[d, i].wait_recv()
            mine, rest = slice(PA * d, PA * d + PA), slice(PA - PA * d, PB - PA * d)
            st2[d, i, mine] = (part[i, t, mine] + r1[d, i].astype(F32)).astype(BF16)
            st2[d, i, rest] = part[i, t, rest].astype(BF16)
            ry2_c[d, i] = send(st2.at[d, i], r2.at[d, i], ry2, (d, i), ydir[d])

    def step3(i):
        recv_both(ry2_c, i)
        red[i] = part[i, 3, 0:PB] + (r2[0, i].astype(F32) + r2[1, i].astype(F32))

    def chain(s):
        for d, idx in ((0, up_of), (1, dn_of)):
            i = idx[s]
            mine = slice(PA * d, PA * d + PA)
            if s == 0:
                zst[d, 0, mine] = red[i, mine].astype(BF16)
                blk = pl.ds(PA * d, PA)
                rz_c[d, s] = send(zst.at[d, 0, blk], zr.at[d, 0, blk], rz, (d, s), zdir[d])
                continue
            rz_c[d, s - 1].wait_recv()
            if s == 1:
                rest = slice(PA - PA * d, PB - PA * d)
                zst[d, s, mine] = (red[i, mine] + zr[d, 0, mine].astype(F32)).astype(BF16)
                zst[d, s, rest] = red[i, rest].astype(BF16)
            else:
                zst[d, s] = (red[i] + zr[d, s - 1].astype(F32)).astype(BF16)
            rz_c[d, s] = send(zst.at[d, s], zr.at[d, s], rz, (d, s), zdir[d])

    def chain_end():
        recv_both(rz_c, 3)
        total = red[7] + (zr[0, 3].astype(F32) + zr[1, 3].astype(F32))
        gw[0:PB] = total * GRADW_SCALE

    def qchain(b, s):
        ys = pl.ds(2 * b, 2)
        for d, idx in ((0, up_of), (1, dn_of)):
            i = idx[s]
            term = part[i, 2 * b : 2 * b + 2, PB:ROWS]
            if s > 0:
                qz_c[b, d, s - 1].wait_recv()
            if s == 0:
                t = 2 * b + d
                qst[d, 0, t] = part[i, t, PB:ROWS].astype(BF16)
                blk = pl.ds(t, 1)
                qz_c[b, d, s] = send(qst.at[d, 0, blk], qr.at[d, 0, blk], qz, (b, d, s), zdir[d])
                continue
            if s == 1:
                t, u = 2 * b + d, 2 * b + 1 - d
                qst[d, s, t] = (part[i, t, PB:ROWS] + qr[d, 0, t].astype(F32)).astype(BF16)
                qst[d, s, u] = part[i, u, PB:ROWS].astype(BF16)
            else:
                got = qr[d, s - 1, 2 * b : 2 * b + 2].astype(F32)
                qst[d, s, 2 * b : 2 * b + 2] = (term + got).astype(BF16)
            qz_c[b, d, s] = send(qst.at[d, s, ys], qr.at[d, s, ys], qz, (b, d, s), zdir[d])

    def q_sum(b):
        for d in (0, 1):
            qz_c[b, d, 3].wait_recv()
        ys = slice(2 * b, 2 * b + 2)
        got = qr[0, 3, ys].astype(F32) + qr[1, 3, ys].astype(F32)
        part[7, ys, PB:ROWS] = part[7, ys, PB:ROWS] + got

    def q_y1():
        q_sum(0)
        for d in (0, 1):
            qy1s[d] = part[7, 0, PB:ROWS, 512 * d : 512 * d + 512].astype(BF16)
            qya_c[d] = send(qy1s.at[d], qy1r.at[d], qya, (d,), ydir[d])

    def q_y2():
        q_sum(1)
        for d in (0, 1):
            t = y_of[d]
            qya_c[d].wait_recv()
            mine = slice(512 * d, 512 * d + 512)
            rest = slice(512 - 512 * d, 1024 - 512 * d)
            qy2s[d, :, mine] = (part[7, t, PB:ROWS, mine] + qy1r[d].astype(F32)).astype(BF16)
            qy2s[d, :, rest] = part[7, t, PB:ROWS, rest].astype(BF16)
            qyb_c[d] = send(qy2s.at[d], qy2r.at[d], qyb, (d,), ydir[d])

    def q_end():
        for d in (0, 1):
            qyb_c[d].wait_recv()
        total = part[7, 3, PB:ROWS] + (qy2r[0].astype(F32) + qy2r[1].astype(F32))
        gw[PB:ROWS] = total * GRADW_SCALE

    stores = []

    def store(i, src_ref, dst_ref):
        copy = pltpu.make_async_copy(src_ref, dst_ref, store_sem.at[i])
        copy.start()
        stores.append(copy)

    half8 = ((0, 4), (4, 4))
    nsib_c = []

    def norm(n):
        for_heads(*half8[n], norm_head, 4)
        blk = pl.ds(512 * n, 512)
        src, dst = normed.at[pl.ds(0, BLK), blk], normed.at[pl.ds(BLK, BLK), blk]
        nsib_c.append(send(src, dst, nsib, (n,), {"c": other}))

    def cot_wait():
        for copy in cot2:
            copy.wait_recv()

    def sib_wait():
        for copy in nsib_c:
            copy.wait_recv()
        for copy in tsib_c.values():
            copy.wait_recv()

    def local_grad(n):
        for_heads(*half8[n], local_grad_head, 4)
        if n == 1:
            store(0, gq, gq_hbm)

    def final_grad():
        for_heads(0, 8, final_grad_head, 4)
        store(1, gk, gk_hbm)
        store(2, gv, gv_hbm)

    loads[1].wait()
    ag_start()
    scan_start(0)
    turn(0)
    scan_a(0)
    ag_q1()
    ag_p(1)
    send_zq(0, 1)
    forward_yp(0)
    ag_q2()
    forward_yp(1)
    send_zq(1, 1)
    send_zq(2, 1)
    forward_yp(2)
    send_sib(0)
    ag_p(2)
    scan_c(0)
    cot_forward()
    send_zq(0, 2)
    turn(2)
    send_zq(3, 1)
    send_zq(1, 2)
    send_sib(1)
    send_sib(2)
    turn(1)
    send_zq(2, 2)
    forward_yp(3)
    ag_p(3)
    forward_yp(4)
    cot_wait()
    d_attn((0, 1, 2), True)
    send_zq(3, 2)
    send_sib(3)
    send_zq(0, 3)
    send_zq(1, 3)
    forward_yp(5)
    scan_e(0)
    forward_yp(6)
    send_zq(2, 3)
    ag_p(4)
    send_sib(4)
    turn(3)
    scan_end(0)
    norm(0)
    send_zq(3, 3)
    norm(1)
    send_sib(6)
    send_sib(5)
    d_attn((3, 4))
    forward_yp(7)
    sib_wait()
    product(0, 1)
    qchain(0, 0)
    step1(0)
    qchain(1, 0)
    product(1, 3)
    step1(2)
    step1(1)
    d_attn((5, 6))
    send_sib(7)
    step2(0)
    qchain(0, 1)
    qchain(1, 1)
    product(3, 5)
    d_attn((7,))
    for_heads(0, 8, draw_head, 4)
    scan_start(1)
    step1(4)
    qchain(0, 2)
    step2(1)
    step3(0)
    chain(0)
    step2(2)
    scan_a(1)
    step1(3)
    qchain(1, 2)
    product(5, 8)
    step1(6)
    step2(4)
    step1(5)
    step3(1)
    step1(7)
    qchain(0, 3)
    local_grad(0)
    step3(2)
    chain(1)
    local_grad(1)
    step2(3)
    step2(6)
    qchain(1, 3)
    step3(4)
    q_y1()
    scan_c(1)
    step2(5)
    step2(7)
    step3(3)
    chain(2)
    step3(6)
    q_y2()
    step3(5)
    chain(3)
    step3(7)
    scan_e(1)
    q_end()
    scan_end(1)
    final_grad()
    chain_end()
    store(3, gw, gw_hbm)
    for copy in stores:
        copy.wait()
    for copy in pending:
        copy.wait_send()


def handed_out(*refs):
    ins, outs, held, sems = refs[:4], refs[4:8], refs[8:12], refs[12]
    into = [pltpu.make_async_copy(a, b, sems.at[0, i]) for i, (a, b) in enumerate(zip(ins, held))]
    back = [pltpu.make_async_copy(a, b, sems.at[1, i]) for i, (a, b) in enumerate(zip(held, outs))]
    for copy in into:
        copy.start()
    for i in range(4):
        into[i].wait()
        back[i].start()
    for copy in back:
        copy.wait()


def body(query_act, key_act, value_act, out_weight, out_cotangent):
    vm = pltpu.VMEM
    dma = pltpu.SemaphoreType.DMA
    state = (HDIM, HDIM)
    scratch = [
        vm((BLK, WIDTH), BF16), vm((BLK, WIDTH), BF16), vm((BLK, WIDTH), BF16),
        vm((NZ, NY, NC, ROWS, WIDTH), BF16),
        vm((NX, BLK, COLS), BF16),
        vm((NZ, NY, ROWS, 2 * BLK), BF16), vm((NZ, NY, ROWS, BLK), BF16),
        vm((2 * BLK, WIDTH), BF16),
        vm((HEADS, BLK, BLK), BF16),
        vm((BLK, WIDTH), F32),
        vm((HEADS, BLK, 1), F32),
        vm((BLK, WIDTH), F32),
        vm((BLK, WIDTH), BF16),
        vm((BLK, WIDTH), F32), vm((BLK, WIDTH), F32),
        vm((BLK, WIDTH), BF16), vm((BLK, WIDTH), BF16), vm((BLK, WIDTH), BF16),
        vm((ROWS, WIDTH), F32),
        vm((NZ, NY, ROWS, WIDTH), F32),
        vm((8, PB, WIDTH), BF16), vm((2, 8, PA, WIDTH), BF16),
        vm((2, 8, PB, WIDTH), BF16), vm((2, 8, PB, WIDTH), BF16),
        vm((8, PB, WIDTH), F32),
        vm((2, 4, PB, WIDTH), BF16), vm((2, 4, PB, WIDTH), BF16),
        vm((2, 4, NY, PA, WIDTH), BF16), vm((2, 4, NY, PA, WIDTH), BF16),
        vm((2, PA, 512), BF16), vm((2, PA, 512), BF16),
        vm((2, PA, WIDTH), BF16), vm((2, PA, WIDTH), BF16),
        vm((2, HEADS, *state), F32),
        vm((2, 4, *state), BF16), vm((2, 4, *state), BF16),
        vm((2, CHIPS, 16, HDIM), BF16), vm((2, CHIPS, 16, HDIM), BF16),
        vm((2, CHIPS, 16, HDIM), BF16), vm((2, CHIPS, 16, HDIM), BF16),
        vm((2, 4, *state), BF16), vm((2, HEADS, *state), BF16),
        dma((5,)), dma((4,)), dma((2, 2)), dma((2, 2)),
        dma((2, 2, 4)), dma((2, 2, 8)), dma((2, 2, 8)),
        dma((2, 2)), dma((2, 2)), dma((2, 4, 2, 4)),
        dma((2, 8)), dma((2, 4, 2)), dma((2, 2)),
        dma((2, 2, 8)), dma((2, 2, 8)), dma((2, 2, 4)), dma((2, 2, 2, 4)),
        dma((2, 2)), dma((2, 2)),
        dma((2, 2)), dma((2, 2)), dma((2, 2)), dma((2, 2)),
    ]
    grad = jax.ShapeDtypeStruct((BLK, WIDTH), BF16)
    shapes = (grad, grad, grad, jax.ShapeDtypeStruct((ROWS, WIDTH), F32))
    anywhere = pl.BlockSpec(memory_space=pl.ANY)
    made = pl.pallas_call(
        kernel,
        out_shape=shapes,
        in_specs=[anywhere] * 5,
        out_specs=[anywhere] * 4,
        scratch_shapes=scratch,
        compiler_params=pltpu.CompilerParams(
            collective_id=0, has_side_effects=True, vmem_limit_bytes=56 * 1024 * 1024
        ),
        name="layer_backward",
    )(query_act, key_act, value_act, out_weight, out_cotangent)
    return pl.pallas_call(
        handed_out,
        out_shape=shapes,
        in_specs=[anywhere] * 4,
        out_specs=[anywhere] * 4,
        scratch_shapes=[*(vm(s.shape, s.dtype) for s in shapes), dma((2, 4))],
        name="hand_out",
    )(*made)


def solution(mesh):
    finer = Mesh(mesh.devices.reshape(NZ, NY, NC, NX), ("z", "y", "c", "x"))
    spec = P(("z", "y", "c"), "x")
    return jax.shard_map(
        body, mesh=finer, in_specs=(spec,) * 5, out_specs=(spec,) * 4, check_vma=False
    )
```

```python
import functools

import jax
import jax.numpy as jnp
from jax import lax
from jax.experimental import pallas as pl
from jax.experimental.pallas import tpu as pltpu
from jax.sharding import Mesh
from jax.sharding import PartitionSpec as P

HDIM = 128
BLK = 256
EPS = 1e-06
NZ, NY, NC, NX = 8, 4, 2, 4
CHIPS = NZ * NY
HEADS = 8
ROWS = 48
WIDTH = 1024
COLS = 768
SLAB = NY * NC * ROWS
PA = 16
PB = 32
F32 = jnp.float32
BF16 = jnp.bfloat16
GRADW_SCALE = 1.0 / 128.0


def dot_nn(a, b):
    return lax.dot_general(a, b, (((1,), (0,)), ((), ())), preferred_element_type=F32)


def dot_nt(a, b):
    return lax.dot_general(a, b, (((1,), (1,)), ((), ())), preferred_element_type=F32)


def dot_tn(a, b):
    return lax.dot_general(a, b, (((0,), (0,)), ((), ())), preferred_element_type=F32)


def kernel(
    q_hbm, k_hbm, v_hbm, w_hbm, cot_hbm,
    gq, gk, gv, gw,
    q, k, v, wb, cot, cot_t, cot_o, normed, scores, raw, inv, da, draw, pk, pv,
    part, st1, r1, st2, r2, red, zst, zr, qst, qr, qy1s, qy1r, qy2s, qy2r,
    own, s_send, s_recv, a_send, a_recv, c_send, c_recv, e_send, e_recv,
    line_sem, load_sem, cx1, cx2, zp_sem, yp1, yp2, qy1, qy2, zq, sib, tsib, nsib,
    ry1, ry2, rz, qz, qya, qyb, ss, sa, sc, se,
):
    z, y, c, x = (lax.axis_index(n) for n in ("z", "y", "c", "x"))
    up_z, dn_z = lax.rem(z + 1, NZ), lax.rem(z + NZ - 1, NZ)
    up_y, dn_y, far_y = lax.rem(y + 1, NY), lax.rem(y + 3, NY), lax.rem(y + 2, NY)
    up_x, dn_x, far_x = lax.rem(x + 1, NX), lax.rem(x + 3, NX), lax.rem(x + 2, NX)
    other = 1 - c
    zdir = ({"z": up_z}, {"z": dn_z})
    ydir = ({"y": up_y}, {"y": dn_y})
    xdir = ({"x": up_x}, {"x": dn_x})
    pending = []

    def send(src, dst, sems, at, device):
        copy = pltpu.make_async_remote_copy(
            src_ref=src, dst_ref=dst, send_sem=sems.at[(0, *at)], recv_sem=sems.at[(1, *at)],
            device_id=device, device_id_type=pl.DeviceIdType.MESH,
        )
        copy.start()
        pending.append(copy)
        return copy

    loads = [
        pltpu.make_async_copy(src, dst, load_sem.at[i])
        for i, (src, dst) in enumerate(
            ((cot_hbm, cot.at[x]), (w_hbm, wb.at[z, y, c]), (k_hbm, k), (v_hbm, v), (q_hbm, q))
        )
    ]
    for load in loads:
        load.start()

    chip = z * NY + y

    def chip_peer(o):
        t = lax.rem(chip + o, CHIPS)
        return t, {"z": lax.div(t, NY), "y": lax.rem(t, NY)}

    barrier = pltpu.get_barrier_semaphore()

    def greet(peer):
        pl.semaphore_signal(barrier, inc=1, device_id=peer, device_id_type=pl.DeviceIdType.MESH)

    near = [{"c": other}, *xdir]
    near += [{"y": lax.rem(y + o, NY)} for o in range(1, NY)]
    near += [{"z": lax.rem(z + o, NZ)} for o in range(1, NZ)]
    for peer in near:
        greet(peer)

    def cols_of(h):
        return pl.ds(pl.multiple_of(h * HDIM, HDIM), HDIM)

    def for_heads(first, count, fn, unroll=2):
        @pl.loop(0, count // unroll)
        def _(i):
            for u in range(unroll):
                fn(first + i * unroll + u)

    mask = (
        lax.broadcasted_iota(jnp.int32, (BLK, BLK), 0)
        >= lax.broadcasted_iota(jnp.int32, (BLK, BLK), 1)
    )

    def kv_head(h):
        cs = cols_of(h)
        own[0, h] = dot_tn(k[:, cs], v[:, cs])

    def score_head(h):
        cs = cols_of(h)
        s = jnp.where(mask, dot_nt(q[:, cs], k[:, cs]), 0.0).astype(BF16)
        scores[h] = s
        raw[:, cs] = dot_nn(s, v[:, cs])

    def norm_head(h):
        cs = cols_of(h)
        r = raw[:, cs] + dot_nn(q[:, cs], e_recv[0, h])
        i = lax.rsqrt(jnp.mean(r * r, axis=-1, keepdims=True) + EPS)
        a = r * i
        raw[:, cs] = a
        inv[h] = i
        normed[0:BLK, cs] = a.astype(BF16)

    def draw_head(h):
        cs = cols_of(h)
        d, a = da[:, cs], raw[:, cs]
        center = jnp.mean(d * a, axis=-1, keepdims=True)
        dr = (inv[h] * (d - a * center)).astype(BF16)
        draw[:, cs] = dr
        own[1, h] = dot_tn(q[:, cs], dr)

    def local_grad_head(h):
        cs = cols_of(h)
        dr = draw[:, cs]
        ds = jnp.where(mask, dot_nt(dr, v[:, cs]), 0.0).astype(BF16)
        gq[:, cs] = (dot_nn(ds, k[:, cs]) + dot_nt(dr, e_recv[0, h])).astype(BF16)
        pk[:, cs] = dot_tn(ds, q[:, cs])
        pv[:, cs] = dot_tn(scores[h], dr)

    def final_grad_head(h):
        cs = cols_of(h)
        gk[:, cs] = (pk[:, cs] + dot_nt(v[:, cs], e_recv[1, h])).astype(BF16)
        gv[:, cs] = (pv[:, cs] + dot_nn(k[:, cs], e_recv[1, h])).astype(BF16)

    for i in (2, 3):
        loads[i].wait()
    for_heads(0, 8, kv_head, 4)
    loads[4].wait()
    for_heads(0, 8, score_head, 4)
    pl.semaphore_wait(barrier, len(near))
    for o in range(1, NY):
        dev = {"y": lax.rem(y + o, NY)}
        pl.semaphore_signal(line_sem, inc=1, device_id=dev, device_id_type=pl.DeviceIdType.MESH)

    loads[0].wait()
    cot1 = [send(cot.at[x], cot.at[x], cx1, (d,), xdir[d]) for d in (0, 1)]
    cot2 = []

    def cot_forward():
        cot1[0].wait_recv()
        half = cot.at[dn_x, pl.ds(0, 128)]
        cot2.append(send(half, half, cx2, (0,), xdir[0]))
        cot1[1].wait_recv()
        half = cot.at[up_x, pl.ds(128, 128)]
        cot2.append(send(half, half, cx2, (1,), xdir[1]))

    ag_z = [lax.rem(z + NZ + o, NZ) for o in (0, -1, 1, -2, 2, -3, 3, 4)]
    zp_c, yp1_c, yp2_c, qy1_c, qy2_c, zq_c, sib_c = {}, {}, {}, {}, {}, {}, {}

    def send_zp(r):
        for d, org in ((0, lax.rem(z + NZ - r, NZ)), (1, lax.rem(z + r, NZ))):
            rows = pl.ds(0, PB) if r < 3 else pl.ds(PA * d, PA)
            blk = wb.at[org, y, c, rows]
            zp_c[d, r] = send(blk, blk, zp_sem, (d, r), zdir[d])

    def send_yp1(i):
        for d in (0, 1):
            blk = wb.at[ag_z[i], y, c, pl.ds(0, PB)]
            yp1_c[d, i] = send(blk, blk, yp1, (d, i), ydir[d])

    def forward_yp(i):
        for d, org in ((0, dn_y), (1, up_y)):
            yp1_c[d, i].wait_recv()
            blk = wb.at[ag_z[i], org, c, pl.ds(PA * d, PA)]
            yp2_c[d, i] = send(blk, blk, yp2, (d, i), ydir[d])

    def send_qy1():
        for d in (0, 1):
            blk = wb.at[z, y, c, pl.ds(PB, PA)]
            qy1_c[d] = send(blk, blk, qy1, (d,), ydir[d])

    def forward_qy():
        for d, org in ((0, dn_y), (1, up_y)):
            qy1_c[d].wait_recv()
            blk = wb.at[z, org, c, pl.ds(PB, PA), pl.ds(512 * d, 512)]
            qy2_c[d] = send(blk, blk, qy2, (d,), ydir[d])

    q_rows = (y, dn_y, up_y, far_y)

    def send_zq(b, r):
        if r > 0:
            for d in (0, 1):
                zq_c[b, d, r - 1].wait_recv()
        for d, org in ((0, lax.rem(z + NZ - r, NZ)), (1, lax.rem(z + r, NZ))):
            lanes = pl.ds(0, WIDTH) if r < 3 else pl.ds(512 * d, 512)
            blk = wb.at[org, q_rows[b], c, pl.ds(PB, PA), lanes]
            zq_c[b, d, r] = send(blk, blk, zq, (b, d, r), zdir[d])

    def recv_both(copies, r):
        for d in (0, 1):
            copies[d, r].wait_recv()

    def ag_start():
        send_zp(0)
        send_qy1()
        send_zq(0, 0)
        send_yp1(0)

    def ag_q1():
        forward_qy()
        send_zq(1, 0)
        send_zq(2, 0)

    def ag_q2():
        qy2_c[0].wait_recv()
        qy2_c[1].wait_recv()
        send_zq(3, 0)

    def ag_p(r):
        recv_both(zp_c, r - 1)
        if r < 4:
            send_zp(r)
            send_yp1(2 * r - 1)
            send_yp1(2 * r)
        else:
            send_yp1(7)

    def send_sib(i):
        recv_both(yp2_c, i)
        if i == 7:
            for b in range(4):
                zq_c[b, 0, 3].wait_recv()
                zq_c[b, 1, 3].wait_recv()
        blk = wb.at[ag_z[i], :, c]
        sib_c[i] = send(blk, blk, sib, (i,), {"c": other})

    order = (range(CHIPS), range(CHIPS - 1, -1, -1))
    s_c, e_c = {}, {}
    mine4, rest4 = pl.ds(c * 4, 4), pl.ds(other * 4, 4)
    state4 = (4, HDIM, HDIM)

    def spread(src, dst, sem, s):
        @pl.loop(1, CHIPS)
        def _(o):
            t, dev = chip_peer(o)
            pltpu.make_async_remote_copy(
                src_ref=src.at[s, t], dst_ref=dst.at[s, chip],
                send_sem=sem.at[0, s], recv_sem=sem.at[1, s],
                device_id=dev, device_id_type=pl.DeviceIdType.MESH,
            ).start()

        dst[s, chip] = src[s, chip]
        all_but_one = pl.ds(0, CHIPS - 1)
        whole = pltpu.make_async_remote_copy(
            src_ref=src.at[s, all_but_one], dst_ref=dst.at[s, all_but_one],
            send_sem=sem.at[0, s], recv_sem=sem.at[1, s],
            device_id=chip_peer(1)[1], device_id_type=pl.DeviceIdType.MESH,
        )
        pending.append(whole)
        return whole

    a_c, c_c = {}, {}

    def scan_start(s):
        s_send[s] = own[s, rest4].astype(BF16)
        s_c[s] = send(s_send.at[s], s_recv.at[s], ss, (s,), {"c": other})

    def scan_a(s):
        s_c[s].wait_recv()
        total = own[s, mine4] + s_recv[s].astype(F32)
        a_send[s] = total.astype(BF16).reshape(CHIPS, 16, HDIM)
        if s == 0:
            pl.semaphore_wait(line_sem, NY - 1)
        a_c[s] = spread(a_send, a_recv, sa, s)

    def scan_c(s):
        a_c[s].wait_recv()
        run = jnp.zeros((16, HDIM), F32)
        for t in order[s]:
            c_send[s, t] = run.astype(BF16)
            run = run + a_recv[s, t].astype(F32)
        c_c[s] = spread(c_send, c_recv, sc, s)

    def scan_e(s):
        c_c[s].wait_recv()
        first = c == s
        outer = c_recv[s].reshape(state4).astype(F32)
        after_own = outer + own[s, mine4]
        after_sib = outer + s_recv[s].astype(F32)
        e_send[s] = jnp.where(first, after_own, outer).astype(BF16)
        e_c[s] = send(e_send.at[s], e_recv.at[s, mine4], se, (s,), {"c": other})
        e_recv[s, mine4] = jnp.where(first, outer, after_sib).astype(BF16)

    def scan_end(s):
        e_c[s].wait_recv()

    x_order = (x, dn_x, up_x, far_x)
    tsib_c = {}

    def turn(i):
        xo = x_order[i]
        for half in (0, 1):
            far_first = lax.rem(xo * 2 + half - z + NZ, NZ)
            zi = jnp.where(far_first < 4, 7 - 2 * far_first, 2 * far_first - 8)
            t = cot[xo, :, pl.ds(half * SLAB, SLAB)].T.reshape(NY, NC, ROWS, BLK)
            for yt in range(NY):
                dy = lax.rem(yt - y + NY, NY)
                yi = jnp.where(dy == 0, 3, jnp.where(dy == 2, 0, jnp.where(dy == 1, 1, 2)))
                keep = jnp.where(c == 0, t[yt, 0], t[yt, 1])
                give = jnp.where(c == 0, t[yt, 1], t[yt, 0])
                cot_t[zi, yi, :, 0:BLK] = keep
                cot_o[zi, yi] = give
            tsib_c[i, half] = send(
                cot_o.at[zi], cot_t.at[zi, :, :, pl.ds(BLK, BLK)], tsib, (i, half), {"c": other}
            )

    def d_attn(idx, first=False):
        for i in idx:
            sib_c[i].wait_recv()

        @pl.loop(0, 4)
        def _(n):
            cs = pl.ds(pl.multiple_of(n * 256, 256), 256)
            lhs, rhs = [], []
            for i in idx:
                zo = ag_z[i]
                lanes = pl.ds(pl.multiple_of(lax.rem(zo, 2) * SLAB, 128), SLAB)
                lhs.append(cot[lax.div(zo, 2), :, lanes])
                rhs.append(wb[zo, :, :, :, cs].reshape(SLAB, 256))
            t = dot_nn(jnp.concatenate(lhs, 1), jnp.concatenate(rhs, 0))
            da[:, cs] = t if first else da[:, cs] + t

    up_of, dn_of = (0, 1, 3, 5), (0, 2, 4, 6)
    y_of = (1, 2)
    ry1_c, ry2_c, rz_c, qz_c, qya_c, qyb_c = {}, {}, {}, {}, {}, {}

    def product(lo, hi):
        n = hi - lo

        @pl.loop(0, 4)
        def _(col):
            cs = pl.ds(pl.multiple_of(col * 256, 256), 256)
            acc = dot_nn(cot_t[lo:hi].reshape(n * NY * ROWS, 2 * BLK), normed[:, cs])
            part[lo:hi, :, :, cs] = acc.reshape(n, NY, ROWS, 256)

    def step1(i):
        st1[i] = part[i, 0, 0:PB].astype(BF16)
        for d in (0, 1):
            ry1_c[d, i] = send(st1.at[i, pl.ds(PA * d, PA)], r1.at[d, i], ry1, (d, i), ydir[d])

    def step2(i):
        for d in (0, 1):
            t = y_of[d]
            ry1_c[d, i].wait_recv()
            mine, rest = slice(PA * d, PA * d + PA), slice(PA - PA * d, PB - PA * d)
            st2[d, i, mine] = (part[i, t, mine] + r1[d, i].astype(F32)).astype(BF16)
            st2[d, i, rest] = part[i, t, rest].astype(BF16)
            ry2_c[d, i] = send(st2.at[d, i], r2.at[d, i], ry2, (d, i), ydir[d])

    def step3(i):
        recv_both(ry2_c, i)
        red[i] = part[i, 3, 0:PB] + (r2[0, i].astype(F32) + r2[1, i].astype(F32))

    def chain(s):
        for d, idx in ((0, up_of), (1, dn_of)):
            i = idx[s]
            mine = slice(PA * d, PA * d + PA)
            if s == 0:
                zst[d, 0, mine] = red[i, mine].astype(BF16)
                blk = pl.ds(PA * d, PA)
                rz_c[d, s] = send(zst.at[d, 0, blk], zr.at[d, 0, blk], rz, (d, s), zdir[d])
                continue
            rz_c[d, s - 1].wait_recv()
            if s == 1:
                rest = slice(PA - PA * d, PB - PA * d)
                zst[d, s, mine] = (red[i, mine] + zr[d, 0, mine].astype(F32)).astype(BF16)
                zst[d, s, rest] = red[i, rest].astype(BF16)
            else:
                zst[d, s] = (red[i] + zr[d, s - 1].astype(F32)).astype(BF16)
            rz_c[d, s] = send(zst.at[d, s], zr.at[d, s], rz, (d, s), zdir[d])

    def chain_end():
        recv_both(rz_c, 3)
        total = red[7] + (zr[0, 3].astype(F32) + zr[1, 3].astype(F32))
        gw[0:PB] = total * GRADW_SCALE

    def qchain(b, s):
        ys = pl.ds(2 * b, 2)
        for d, idx in ((0, up_of), (1, dn_of)):
            i = idx[s]
            term = part[i, 2 * b : 2 * b + 2, PB:ROWS]
            if s > 0:
                qz_c[b, d, s - 1].wait_recv()
            if s == 0:
                t = 2 * b + d
                qst[d, 0, t] = part[i, t, PB:ROWS].astype(BF16)
                blk = pl.ds(t, 1)
                qz_c[b, d, s] = send(qst.at[d, 0, blk], qr.at[d, 0, blk], qz, (b, d, s), zdir[d])
                continue
            if s == 1:
                t, u = 2 * b + d, 2 * b + 1 - d
                qst[d, s, t] = (part[i, t, PB:ROWS] + qr[d, 0, t].astype(F32)).astype(BF16)
                qst[d, s, u] = part[i, u, PB:ROWS].astype(BF16)
            else:
                got = qr[d, s - 1, 2 * b : 2 * b + 2].astype(F32)
                qst[d, s, 2 * b : 2 * b + 2] = (term + got).astype(BF16)
            qz_c[b, d, s] = send(qst.at[d, s, ys], qr.at[d, s, ys], qz, (b, d, s), zdir[d])

    def q_sum(b):
        for d in (0, 1):
            qz_c[b, d, 3].wait_recv()
        ys = slice(2 * b, 2 * b + 2)
        got = qr[0, 3, ys].astype(F32) + qr[1, 3, ys].astype(F32)
        part[7, ys, PB:ROWS] = part[7, ys, PB:ROWS] + got

    def q_y1():
        q_sum(0)
        for d in (0, 1):
            qy1s[d] = part[7, 0, PB:ROWS, 512 * d : 512 * d + 512].astype(BF16)
            qya_c[d] = send(qy1s.at[d], qy1r.at[d], qya, (d,), ydir[d])

    def q_y2():
        q_sum(1)
        for d in (0, 1):
            t = y_of[d]
            qya_c[d].wait_recv()
            mine = slice(512 * d, 512 * d + 512)
            rest = slice(512 - 512 * d, 1024 - 512 * d)
            qy2s[d, :, mine] = (part[7, t, PB:ROWS, mine] + qy1r[d].astype(F32)).astype(BF16)
            qy2s[d, :, rest] = part[7, t, PB:ROWS, rest].astype(BF16)
            qyb_c[d] = send(qy2s.at[d], qy2r.at[d], qyb, (d,), ydir[d])

    def q_end():
        for d in (0, 1):
            qyb_c[d].wait_recv()
        total = part[7, 3, PB:ROWS] + (qy2r[0].astype(F32) + qy2r[1].astype(F32))
        gw[PB:ROWS] = total * GRADW_SCALE

    half8 = ((0, 4), (4, 4))
    nsib_c = []

    def norm(n):
        for_heads(*half8[n], norm_head, 4)
        blk = pl.ds(512 * n, 512)
        src, dst = normed.at[pl.ds(0, BLK), blk], normed.at[pl.ds(BLK, BLK), blk]
        nsib_c.append(send(src, dst, nsib, (n,), {"c": other}))

    def cot_wait():
        for copy in cot2:
            copy.wait_recv()

    def sib_wait():
        for copy in nsib_c:
            copy.wait_recv()
        for copy in tsib_c.values():
            copy.wait_recv()

    def local_grad(n):
        for_heads(*half8[n], local_grad_head, 4)

    def final_grad():
        for_heads(0, 8, final_grad_head, 4)

    loads[1].wait()
    ag_start()
    scan_start(0)
    turn(0)
    scan_a(0)
    ag_q1()
    ag_p(1)
    send_zq(0, 1)
    forward_yp(0)
    ag_q2()
    forward_yp(1)
    send_zq(1, 1)
    send_zq(2, 1)
    forward_yp(2)
    scan_c(0)
    send_sib(0)
    ag_p(2)
    cot_forward()
    send_zq(0, 2)
    turn(2)
    send_zq(3, 1)
    send_sib(1)
    turn(1)
    send_zq(1, 2)
    send_sib(2)
    send_zq(2, 2)
    forward_yp(3)
    forward_yp(4)
    ag_p(3)
    cot_wait()
    d_attn((0, 1, 2), True)
    send_zq(3, 2)
    scan_e(0)
    send_zq(2, 3)
    send_sib(4)
    send_zq(0, 3)
    send_sib(3)
    ag_p(4)
    send_zq(1, 3)
    forward_yp(5)
    scan_end(0)
    norm(0)
    norm(1)
    turn(3)
    forward_yp(6)
    send_zq(3, 3)
    d_attn((3, 4))
    forward_yp(7)
    sib_wait()
    product(0, 1)
    send_sib(5)
    step1(0)
    qchain(0, 0)
    send_sib(6)
    qchain(1, 0)
    product(1, 3)
    send_sib(7)
    step1(1)
    step1(2)
    product(3, 5)
    qchain(0, 1)
    step1(4)
    qchain(1, 1)
    step2(0)
    d_attn((5, 6))
    d_attn((7,))
    for_heads(0, 8, draw_head, 4)
    scan_start(1)
    qchain(0, 2)
    step1(3)
    step2(1)
    step2(2)
    step3(0)
    chain(0)
    scan_a(1)
    qchain(1, 2)
    product(5, 8)
    qchain(0, 3)
    step1(5)
    step2(3)
    step1(6)
    step3(1)
    step1(7)
    step2(4)
    local_grad(0)
    step3(2)
    chain(1)
    local_grad(1)
    step2(5)
    qchain(1, 3)
    step3(3)
    scan_c(1)
    q_y1()
    step2(6)
    step2(7)
    step3(4)
    chain(2)
    step3(5)
    q_y2()
    step3(6)
    chain(3)
    scan_e(1)
    step3(7)
    q_end()
    scan_end(1)
    final_grad()
    chain_end()
    for copy in pending:
        copy.wait_send()


def handed_out(*refs):
    ins, outs, sems = refs[:4], refs[4:8], refs[8]
    copies = [pltpu.make_async_copy(a, b, sems.at[i]) for i, (a, b) in enumerate(zip(ins, outs))]
    for copy in copies:
        copy.start()
    for copy in copies:
        copy.wait()


def body(query_act, key_act, value_act, out_weight, out_cotangent):
    vm = pltpu.VMEM
    dma = pltpu.SemaphoreType.DMA
    state = (HDIM, HDIM)
    scratch = [
        vm((BLK, WIDTH), BF16), vm((BLK, WIDTH), BF16), vm((BLK, WIDTH), BF16),
        vm((NZ, NY, NC, ROWS, WIDTH), BF16),
        vm((NX, BLK, COLS), BF16),
        vm((NZ, NY, ROWS, 2 * BLK), BF16), vm((NZ, NY, ROWS, BLK), BF16),
        vm((2 * BLK, WIDTH), BF16),
        vm((HEADS, BLK, BLK), BF16),
        vm((BLK, WIDTH), F32),
        vm((HEADS, BLK, 1), F32),
        vm((BLK, WIDTH), F32),
        vm((BLK, WIDTH), BF16),
        vm((BLK, WIDTH), F32), vm((BLK, WIDTH), F32),
        vm((NZ, NY, ROWS, WIDTH), F32),
        vm((8, PB, WIDTH), BF16), vm((2, 8, PA, WIDTH), BF16),
        vm((2, 8, PB, WIDTH), BF16), vm((2, 8, PB, WIDTH), BF16),
        vm((8, PB, WIDTH), F32),
        vm((2, 4, PB, WIDTH), BF16), vm((2, 4, PB, WIDTH), BF16),
        vm((2, 4, NY, PA, WIDTH), BF16), vm((2, 4, NY, PA, WIDTH), BF16),
        vm((2, PA, 512), BF16), vm((2, PA, 512), BF16),
        vm((2, PA, WIDTH), BF16), vm((2, PA, WIDTH), BF16),
        vm((2, HEADS, *state), F32),
        vm((2, 4, *state), BF16), vm((2, 4, *state), BF16),
        vm((2, CHIPS, 16, HDIM), BF16), vm((2, CHIPS, 16, HDIM), BF16),
        vm((2, CHIPS, 16, HDIM), BF16), vm((2, CHIPS, 16, HDIM), BF16),
        vm((2, 4, *state), BF16), vm((2, HEADS, *state), BF16),
        pltpu.SemaphoreType.REGULAR,
        dma((5,)), dma((2, 2)), dma((2, 2)),
        dma((2, 2, 4)), dma((2, 2, 8)), dma((2, 2, 8)),
        dma((2, 2)), dma((2, 2)), dma((2, 4, 2, 4)),
        dma((2, 8)), dma((2, 4, 2)), dma((2, 2)),
        dma((2, 2, 8)), dma((2, 2, 8)), dma((2, 2, 4)), dma((2, 2, 2, 4)),
        dma((2, 2)), dma((2, 2)),
        dma((2, 2)), dma((2, 2)), dma((2, 2)), dma((2, 2)),
    ]
    grad = jax.ShapeDtypeStruct((BLK, WIDTH), BF16)
    shapes = (grad, grad, grad, jax.ShapeDtypeStruct((ROWS, WIDTH), F32))
    far = pl.BlockSpec(memory_space=pltpu.HBM)
    close = pl.BlockSpec(memory_space=pltpu.VMEM)
    ins = [
        pltpu.with_memory_space_constraint(a, pltpu.HBM)
        for a in (query_act, key_act, value_act, out_weight, out_cotangent)
    ]
    made = pl.pallas_call(
        kernel,
        out_shape=shapes,
        in_specs=[far] * 5,
        out_specs=[close] * 4,
        scratch_shapes=scratch,
        compiler_params=pltpu.CompilerParams(
            collective_id=0, has_side_effects=True, vmem_limit_bytes=48 * 1024 * 1024
        ),
        name="layer_backward",
    )(*ins)
    return pl.pallas_call(
        handed_out,
        out_shape=shapes,
        in_specs=[close] * 4,
        out_specs=[far] * 4,
        scratch_shapes=[dma((4,))],
        compiler_params=pltpu.CompilerParams(vmem_limit_bytes=4 * 1024 * 1024),
        name="hand_out",
    )(*made)


def solution(mesh):
    finer = Mesh(mesh.devices.reshape(NZ, NY, NC, NX), ("z", "y", "c", "x"))
    spec = P(("z", "y", "c"), "x")
    return jax.shard_map(
        body, mesh=finer, in_specs=(spec,) * 5, out_specs=(spec,) * 4, check_vma=False
    )
```

```python
import functools

import jax
import jax.numpy as jnp
from jax import lax
from jax.experimental import pallas as pl
from jax.experimental.pallas import tpu as pltpu
from jax.sharding import Mesh
from jax.sharding import PartitionSpec as P

HDIM = 128
BLK = 256
EPS = 1e-06
NZ, NY, NC, NX = 8, 4, 2, 4
CHIPS = NZ * NY
HEADS = 8
ROWS = 48
WIDTH = 1024
COLS = 768
SLAB = NY * NC * ROWS
PA = 16
PB = 32
F32 = jnp.float32
BF16 = jnp.bfloat16
GRADW_SCALE = 1.0 / 128.0


def dot_nn(a, b):
    return lax.dot_general(a, b, (((1,), (0,)), ((), ())), preferred_element_type=F32)


def dot_nt(a, b):
    return lax.dot_general(a, b, (((1,), (1,)), ((), ())), preferred_element_type=F32)


def dot_tn(a, b):
    return lax.dot_general(a, b, (((0,), (0,)), ((), ())), preferred_element_type=F32)


def kernel(
    q_hbm, k_hbm, v_hbm, w_hbm, cot_hbm,
    gq, gk, gv, gw,
    q, k, v, wb, cot, cot_t, cot_o, normed, scores, raw, inv, da, draw, pk, pv,
    part, st1, r1, st2, r2, red, zst, zr, qst, qr, qy1s, qy1r, qy2s, qy2r,
    own, s_send, s_recv, a_send, a_recv, c_send, c_recv, e_send, e_recv,
    line_sem, load_sem, cx1, cx2, zp_sem, yp1, yp2, qy1, qy2, zq, sib, tsib, nsib,
    ry1, ry2, rz, qz, qya, qyb, ss, sa, sc, se,
):
    z, y, c, x = (lax.axis_index(n) for n in ("z", "y", "c", "x"))
    up_z, dn_z = lax.rem(z + 1, NZ), lax.rem(z + NZ - 1, NZ)
    up_y, dn_y, far_y = lax.rem(y + 1, NY), lax.rem(y + 3, NY), lax.rem(y + 2, NY)
    up_x, dn_x, far_x = lax.rem(x + 1, NX), lax.rem(x + 3, NX), lax.rem(x + 2, NX)
    other = 1 - c
    zdir = ({"z": up_z}, {"z": dn_z})
    ydir = ({"y": up_y}, {"y": dn_y})
    xdir = ({"x": up_x}, {"x": dn_x})
    pending = []

    def send(src, dst, sems, at, device):
        copy = pltpu.make_async_remote_copy(
            src_ref=src, dst_ref=dst, send_sem=sems.at[(0, *at)], recv_sem=sems.at[(1, *at)],
            device_id=device, device_id_type=pl.DeviceIdType.MESH,
        )
        copy.start()
        pending.append(copy)
        return copy

    loads = [
        pltpu.make_async_copy(src, dst, load_sem.at[i])
        for i, (src, dst) in enumerate(
            ((cot_hbm, cot.at[x]), (w_hbm, wb.at[z, y, c]), (k_hbm, k), (v_hbm, v), (q_hbm, q))
        )
    ]
    for load in loads:
        load.start()

    chip = z * NY + y

    def chip_peer(o):
        t = lax.rem(chip + o, CHIPS)
        return t, {"z": lax.div(t, NY), "y": lax.rem(t, NY)}

    barrier = pltpu.get_barrier_semaphore()

    def greet(peer):
        pl.semaphore_signal(barrier, inc=1, device_id=peer, device_id_type=pl.DeviceIdType.MESH)

    near = [{"c": other}, *xdir]
    near += [{"y": lax.rem(y + o, NY)} for o in range(1, NY)]
    near += [{"z": lax.rem(z + o, NZ)} for o in range(1, NZ)]
    for peer in near:
        greet(peer)

    def cols_of(h):
        return pl.ds(pl.multiple_of(h * HDIM, HDIM), HDIM)

    def for_heads(first, count, fn, unroll=2):
        @pl.loop(0, count // unroll)
        def _(i):
            for u in range(unroll):
                fn(first + i * unroll + u)

    mask = (
        lax.broadcasted_iota(jnp.int32, (BLK, BLK), 0)
        >= lax.broadcasted_iota(jnp.int32, (BLK, BLK), 1)
    )

    def kv_head(h):
        cs = cols_of(h)
        own[0, h] = dot_tn(k[:, cs], v[:, cs])

    def score_head(h):
        cs = cols_of(h)
        s = jnp.where(mask, dot_nt(q[:, cs], k[:, cs]), 0.0).astype(BF16)
        scores[h] = s
        raw[:, cs] = dot_nn(s, v[:, cs])

    def norm_head(h):
        cs = cols_of(h)
        r = raw[:, cs] + dot_nn(q[:, cs], e_recv[0, h])
        i = lax.rsqrt(jnp.mean(r * r, axis=-1, keepdims=True) + EPS)
        a = r * i
        raw[:, cs] = a
        inv[h] = i
        normed[0:BLK, cs] = a.astype(BF16)

    def draw_head(h):
        cs = cols_of(h)
        d, a = da[:, cs], raw[:, cs]
        center = jnp.mean(d * a, axis=-1, keepdims=True)
        dr = (inv[h] * (d - a * center)).astype(BF16)
        draw[:, cs] = dr
        own[1, h] = dot_tn(q[:, cs], dr)

    def local_grad_head(h):
        cs = cols_of(h)
        dr = draw[:, cs]
        ds = jnp.where(mask, dot_nt(dr, v[:, cs]), 0.0).astype(BF16)
        gq[:, cs] = (dot_nn(ds, k[:, cs]) + dot_nt(dr, e_recv[0, h])).astype(BF16)
        pk[:, cs] = dot_tn(ds, q[:, cs])
        pv[:, cs] = dot_tn(scores[h], dr)

    def final_grad_head(h):
        cs = cols_of(h)
        gk[:, cs] = (pk[:, cs] + dot_nt(v[:, cs], e_recv[1, h])).astype(BF16)
        gv[:, cs] = (pv[:, cs] + dot_nn(k[:, cs], e_recv[1, h])).astype(BF16)

    for i in (2, 3):
        loads[i].wait()
    for_heads(0, 8, kv_head, 8)
    loads[4].wait()
    for_heads(0, 8, score_head, 8)
    pl.semaphore_wait(barrier, len(near))
    for o in range(1, NY):
        dev = {"y": lax.rem(y + o, NY)}
        pl.semaphore_signal(line_sem, inc=1, device_id=dev, device_id_type=pl.DeviceIdType.MESH)

    loads[0].wait()
    cot1 = [send(cot.at[x], cot.at[x], cx1, (d,), xdir[d]) for d in (0, 1)]
    cot2 = []

    def cot_forward():
        cot1[0].wait_recv()
        half = cot.at[dn_x, pl.ds(0, 128)]
        cot2.append(send(half, half, cx2, (0,), xdir[0]))
        cot1[1].wait_recv()
        half = cot.at[up_x, pl.ds(128, 128)]
        cot2.append(send(half, half, cx2, (1,), xdir[1]))

    ag_z = [lax.rem(z + NZ + o, NZ) for o in (0, -1, 1, -2, 2, -3, 3, 4)]
    zp_c, yp1_c, yp2_c, qy1_c, qy2_c, zq_c, sib_c = {}, {}, {}, {}, {}, {}, {}

    def send_zp(r):
        for d, org in ((0, lax.rem(z + NZ - r, NZ)), (1, lax.rem(z + r, NZ))):
            rows = pl.ds(0, PB) if r < 3 else pl.ds(PA * d, PA)
            blk = wb.at[org, y, c, rows]
            zp_c[d, r] = send(blk, blk, zp_sem, (d, r), zdir[d])

    def send_yp1(i):
        for d in (0, 1):
            blk = wb.at[ag_z[i], y, c, pl.ds(0, PB)]
            yp1_c[d, i] = send(blk, blk, yp1, (d, i), ydir[d])

    def forward_yp(i):
        for d, org in ((0, dn_y), (1, up_y)):
            yp1_c[d, i].wait_recv()
            blk = wb.at[ag_z[i], org, c, pl.ds(PA * d, PA)]
            yp2_c[d, i] = send(blk, blk, yp2, (d, i), ydir[d])

    def send_qy1():
        for d in (0, 1):
            blk = wb.at[z, y, c, pl.ds(PB, PA)]
            qy1_c[d] = send(blk, blk, qy1, (d,), ydir[d])

    def forward_qy():
        for d, org in ((0, dn_y), (1, up_y)):
            qy1_c[d].wait_recv()
            blk = wb.at[z, org, c, pl.ds(PB, PA), pl.ds(512 * d, 512)]
            qy2_c[d] = send(blk, blk, qy2, (d,), ydir[d])

    q_rows = (y, dn_y, up_y, far_y)

    def send_zq(b, r):
        if r > 0:
            for d in (0, 1):
                zq_c[b, d, r - 1].wait_recv()
        for d, org in ((0, lax.rem(z + NZ - r, NZ)), (1, lax.rem(z + r, NZ))):
            lanes = pl.ds(0, WIDTH) if r < 3 else pl.ds(512 * d, 512)
            blk = wb.at[org, q_rows[b], c, pl.ds(PB, PA), lanes]
            zq_c[b, d, r] = send(blk, blk, zq, (b, d, r), zdir[d])

    def recv_both(copies, r):
        for d in (0, 1):
            copies[d, r].wait_recv()

    def ag_start():
        send_zp(0)
        send_qy1()
        send_zq(0, 0)
        send_yp1(0)

    def ag_q1():
        forward_qy()
        send_zq(1, 0)
        send_zq(2, 0)

    def ag_q2():
        qy2_c[0].wait_recv()
        qy2_c[1].wait_recv()
        send_zq(3, 0)

    def ag_p(r):
        recv_both(zp_c, r - 1)
        if r < 4:
            send_zp(r)
            send_yp1(2 * r - 1)
            send_yp1(2 * r)
        else:
            send_yp1(7)

    def send_sib(i):
        recv_both(yp2_c, i)
        if i == 7:
            for b in range(4):
                zq_c[b, 0, 3].wait_recv()
                zq_c[b, 1, 3].wait_recv()
        blk = wb.at[ag_z[i], :, c]
        sib_c[i] = send(blk, blk, sib, (i,), {"c": other})

    order = (range(CHIPS), range(CHIPS - 1, -1, -1))
    s_c, e_c = {}, {}
    mine4, rest4 = pl.ds(c * 4, 4), pl.ds(other * 4, 4)
    state4 = (4, HDIM, HDIM)

    def spread(src, dst, sem, s):
        @pl.loop(1, CHIPS)
        def _(o):
            t, dev = chip_peer(o)
            pltpu.make_async_remote_copy(
                src_ref=src.at[s, t], dst_ref=dst.at[s, chip],
                send_sem=sem.at[0, s], recv_sem=sem.at[1, s],
                device_id=dev, device_id_type=pl.DeviceIdType.MESH,
            ).start()

        dst[s, chip] = src[s, chip]
        all_but_one = pl.ds(0, CHIPS - 1)
        whole = pltpu.make_async_remote_copy(
            src_ref=src.at[s, all_but_one], dst_ref=dst.at[s, all_but_one],
            send_sem=sem.at[0, s], recv_sem=sem.at[1, s],
            device_id=chip_peer(1)[1], device_id_type=pl.DeviceIdType.MESH,
        )
        pending.append(whole)
        return whole

    a_c, c_c = {}, {}

    def scan_start(s):
        s_send[s] = own[s, rest4].astype(BF16)
        s_c[s] = send(s_send.at[s], s_recv.at[s], ss, (s,), {"c": other})

    def scan_a(s):
        s_c[s].wait_recv()
        total = own[s, mine4] + s_recv[s].astype(F32)
        a_send[s] = total.astype(BF16).reshape(CHIPS, 16, HDIM)
        if s == 0:
            pl.semaphore_wait(line_sem, NY - 1)
        a_c[s] = spread(a_send, a_recv, sa, s)

    def scan_c(s):
        a_c[s].wait_recv()
        run = jnp.zeros((16, HDIM), F32)
        for t in order[s]:
            c_send[s, t] = run.astype(BF16)
            run = run + a_recv[s, t].astype(F32)
        c_c[s] = spread(c_send, c_recv, sc, s)

    def scan_e(s):
        c_c[s].wait_recv()
        first = c == s
        outer = c_recv[s].reshape(state4).astype(F32)
        after_own = outer + own[s, mine4]
        after_sib = outer + s_recv[s].astype(F32)
        e_send[s] = jnp.where(first, after_own, outer).astype(BF16)
        e_c[s] = send(e_send.at[s], e_recv.at[s, mine4], se, (s,), {"c": other})
        e_recv[s, mine4] = jnp.where(first, outer, after_sib).astype(BF16)

    def scan_end(s):
        e_c[s].wait_recv()

    x_order = (x, dn_x, up_x, far_x)
    tsib_c = {}

    def turn(i):
        xo = x_order[i]
        for half in (0, 1):
            far_first = lax.rem(xo * 2 + half - z + NZ, NZ)
            zi = jnp.where(far_first < 4, 7 - 2 * far_first, 2 * far_first - 8)
            t = cot[xo, :, pl.ds(half * SLAB, SLAB)].T.reshape(NY, NC, ROWS, BLK)
            for yt in range(NY):
                dy = lax.rem(yt - y + NY, NY)
                yi = jnp.where(dy == 0, 3, jnp.where(dy == 2, 0, jnp.where(dy == 1, 1, 2)))
                keep = jnp.where(c == 0, t[yt, 0], t[yt, 1])
                give = jnp.where(c == 0, t[yt, 1], t[yt, 0])
                cot_t[zi, yi, :, 0:BLK] = keep
                cot_o[zi, yi] = give
            tsib_c[i, half] = send(
                cot_o.at[zi], cot_t.at[zi, :, :, pl.ds(BLK, BLK)], tsib, (i, half), {"c": other}
            )

    def d_attn(idx, first=False):
        for i in idx:
            sib_c[i].wait_recv()

        lhs, rhs = [], []
        for i in idx:
            zo = ag_z[i]
            lanes = pl.ds(pl.multiple_of(lax.rem(zo, 2) * SLAB, 128), SLAB)
            lhs.append(cot[lax.div(zo, 2), :, lanes])
            rhs.append(wb[zo].reshape(SLAB, WIDTH))
        t = dot_nn(jnp.concatenate(lhs, 1), jnp.concatenate(rhs, 0))
        da[...] = t if first else da[...] + t

    up_of, dn_of = (0, 1, 3, 5), (0, 2, 4, 6)
    y_of = (1, 2)
    ry1_c, ry2_c, rz_c, qz_c, qya_c, qyb_c = {}, {}, {}, {}, {}, {}

    def product(lo, hi):
        n = hi - lo

        acc = dot_nn(cot_t[lo:hi].reshape(n * NY * ROWS, 2 * BLK), normed[...])
        part[lo:hi] = acc.reshape(n, NY, ROWS, WIDTH)

    def step1(i):
        st1[i] = part[i, 0, 0:PB].astype(BF16)
        for d in (0, 1):
            ry1_c[d, i] = send(st1.at[i, pl.ds(PA * d, PA)], r1.at[d, i], ry1, (d, i), ydir[d])

    def step2(i):
        for d in (0, 1):
            t = y_of[d]
            ry1_c[d, i].wait_recv()
            mine, rest = slice(PA * d, PA * d + PA), slice(PA - PA * d, PB - PA * d)
            st2[d, i, mine] = (part[i, t, mine] + r1[d, i].astype(F32)).astype(BF16)
            st2[d, i, rest] = part[i, t, rest].astype(BF16)
            ry2_c[d, i] = send(st2.at[d, i], r2.at[d, i], ry2, (d, i), ydir[d])

    def step3(i):
        recv_both(ry2_c, i)
        red[i] = part[i, 3, 0:PB] + (r2[0, i].astype(F32) + r2[1, i].astype(F32))

    def chain(s):
        for d, idx in ((0, up_of), (1, dn_of)):
            i = idx[s]
            mine = slice(PA * d, PA * d + PA)
            if s == 0:
                zst[d, 0, mine] = red[i, mine].astype(BF16)
                blk = pl.ds(PA * d, PA)
                rz_c[d, s] = send(zst.at[d, 0, blk], zr.at[d, 0, blk], rz, (d, s), zdir[d])
                continue
            rz_c[d, s - 1].wait_recv()
            if s == 1:
                rest = slice(PA - PA * d, PB - PA * d)
                zst[d, s, mine] = (red[i, mine] + zr[d, 0, mine].astype(F32)).astype(BF16)
                zst[d, s, rest] = red[i, rest].astype(BF16)
            else:
                zst[d, s] = (red[i] + zr[d, s - 1].astype(F32)).astype(BF16)
            rz_c[d, s] = send(zst.at[d, s], zr.at[d, s], rz, (d, s), zdir[d])

    def chain_end():
        recv_both(rz_c, 3)
        total = red[7] + (zr[0, 3].astype(F32) + zr[1, 3].astype(F32))
        gw[0:PB] = total * GRADW_SCALE

    def qchain(b, s):
        ys = pl.ds(2 * b, 2)
        for d, idx in ((0, up_of), (1, dn_of)):
            i = idx[s]
            term = part[i, 2 * b : 2 * b + 2, PB:ROWS]
            if s > 0:
                qz_c[b, d, s - 1].wait_recv()
            if s == 0:
                t = 2 * b + d
                qst[d, 0, t] = part[i, t, PB:ROWS].astype(BF16)
                blk = pl.ds(t, 1)
                qz_c[b, d, s] = send(qst.at[d, 0, blk], qr.at[d, 0, blk], qz, (b, d, s), zdir[d])
                continue
            if s == 1:
                t, u = 2 * b + d, 2 * b + 1 - d
                qst[d, s, t] = (part[i, t, PB:ROWS] + qr[d, 0, t].astype(F32)).astype(BF16)
                qst[d, s, u] = part[i, u, PB:ROWS].astype(BF16)
            else:
                got = qr[d, s - 1, 2 * b : 2 * b + 2].astype(F32)
                qst[d, s, 2 * b : 2 * b + 2] = (term + got).astype(BF16)
            qz_c[b, d, s] = send(qst.at[d, s, ys], qr.at[d, s, ys], qz, (b, d, s), zdir[d])

    def q_sum(b):
        for d in (0, 1):
            qz_c[b, d, 3].wait_recv()
        ys = slice(2 * b, 2 * b + 2)
        got = qr[0, 3, ys].astype(F32) + qr[1, 3, ys].astype(F32)
        part[7, ys, PB:ROWS] = part[7, ys, PB:ROWS] + got

    def q_y1():
        q_sum(0)
        for d in (0, 1):
            qy1s[d] = part[7, 0, PB:ROWS, 512 * d : 512 * d + 512].astype(BF16)
            qya_c[d] = send(qy1s.at[d], qy1r.at[d], qya, (d,), ydir[d])

    def q_y2():
        q_sum(1)
        for d in (0, 1):
            t = y_of[d]
            qya_c[d].wait_recv()
            mine = slice(512 * d, 512 * d + 512)
            rest = slice(512 - 512 * d, 1024 - 512 * d)
            qy2s[d, :, mine] = (part[7, t, PB:ROWS, mine] + qy1r[d].astype(F32)).astype(BF16)
            qy2s[d, :, rest] = part[7, t, PB:ROWS, rest].astype(BF16)
            qyb_c[d] = send(qy2s.at[d], qy2r.at[d], qyb, (d,), ydir[d])

    def q_end():
        for d in (0, 1):
            qyb_c[d].wait_recv()
        total = part[7, 3, PB:ROWS] + (qy2r[0].astype(F32) + qy2r[1].astype(F32))
        gw[PB:ROWS] = total * GRADW_SCALE

    half8 = ((0, 4), (4, 4))
    nsib_c = []

    def norm(n):
        for_heads(*half8[n], norm_head, 4)
        blk = pl.ds(512 * n, 512)
        src, dst = normed.at[pl.ds(0, BLK), blk], normed.at[pl.ds(BLK, BLK), blk]
        nsib_c.append(send(src, dst, nsib, (n,), {"c": other}))

    def cot_wait():
        for copy in cot2:
            copy.wait_recv()

    def sib_wait():
        for copy in nsib_c:
            copy.wait_recv()
        for copy in tsib_c.values():
            copy.wait_recv()

    def local_grad(n):
        for_heads(*half8[n], local_grad_head, 4)

    def final_grad():
        for_heads(0, 8, final_grad_head, 8)

    loads[1].wait()
    ag_start()
    scan_start(0)
    turn(0)
    scan_a(0)
    ag_q1()
    ag_p(1)
    send_zq(0, 1)
    forward_yp(0)
    ag_q2()
    forward_yp(1)
    send_zq(1, 1)
    send_zq(2, 1)
    forward_yp(2)
    scan_c(0)
    send_sib(0)
    ag_p(2)
    cot_forward()
    turn(1)
    send_zq(3, 1)
    send_sib(1)
    turn(2)
    send_sib(2)
    send_zq(1, 2)
    send_zq(2, 2)
    send_zq(0, 2)
    forward_yp(3)
    forward_yp(4)
    ag_p(3)
    cot_wait()
    d_attn((0, 1, 2), True)
    scan_e(0)
    send_zq(1, 3)
    send_zq(3, 2)
    send_sib(3)
    turn(3)
    send_zq(0, 3)
    scan_end(0)
    norm(0)
    ag_p(4)
    norm(1)
    forward_yp(5)
    send_sib(4)
    send_zq(2, 3)
    send_zq(3, 3)
    forward_yp(6)
    sib_wait()
    product(0, 1)
    step1(0)
    qchain(0, 0)
    qchain(1, 0)
    d_attn((3, 4))
    forward_yp(7)
    product(1, 3)
    send_sib(5)
    step1(2)
    step1(1)
    send_sib(6)
    product(3, 5)
    step2(0)
    qchain(0, 1)
    step1(3)
    step1(4)
    send_sib(7)
    qchain(1, 1)
    product(5, 8)
    step2(2)
    step1(6)
    d_attn((5, 6))
    d_attn((7,))
    for_heads(0, 8, draw_head, 8)
    scan_start(1)
    qchain(0, 2)
    step3(0)
    chain(0)
    step2(1)
    step2(4)
    scan_a(1)
    qchain(1, 2)
    step2(3)
    step3(2)
    step1(5)
    local_grad(0)
    local_grad(1)
    qchain(0, 3)
    step3(1)
    chain(1)
    step2(6)
    step1(7)
    step3(4)
    qchain(1, 3)
    step3(3)
    step2(5)
    scan_c(1)
    q_y1()
    step3(6)
    chain(2)
    step2(7)
    step3(5)
    q_y2()
    step3(7)
    chain(3)
    scan_e(1)
    q_end()
    scan_end(1)
    final_grad()
    chain_end()
    for copy in pending:
        copy.wait_send()


def handed_out(*refs):
    ins, outs, sems = refs[:4], refs[4:8], refs[8]
    copies = [pltpu.make_async_copy(a, b, sems.at[i]) for i, (a, b) in enumerate(zip(ins, outs))]
    for copy in copies:
        copy.start()
    for copy in copies:
        copy.wait()


def body(query_act, key_act, value_act, out_weight, out_cotangent):
    vm = pltpu.VMEM
    dma = pltpu.SemaphoreType.DMA
    state = (HDIM, HDIM)
    scratch = [
        vm((BLK, WIDTH), BF16), vm((BLK, WIDTH), BF16), vm((BLK, WIDTH), BF16),
        vm((NZ, NY, NC, ROWS, WIDTH), BF16),
        vm((NX, BLK, COLS), BF16),
        vm((NZ, NY, ROWS, 2 * BLK), BF16), vm((NZ, NY, ROWS, BLK), BF16),
        vm((2 * BLK, WIDTH), BF16),
        vm((HEADS, BLK, BLK), BF16),
        vm((BLK, WIDTH), F32),
        vm((HEADS, BLK, 1), F32),
        vm((BLK, WIDTH), F32),
        vm((BLK, WIDTH), BF16),
        vm((BLK, WIDTH), F32), vm((BLK, WIDTH), F32),
        vm((NZ, NY, ROWS, WIDTH), F32),
        vm((8, PB, WIDTH), BF16), vm((2, 8, PA, WIDTH), BF16),
        vm((2, 8, PB, WIDTH), BF16), vm((2, 8, PB, WIDTH), BF16),
        vm((8, PB, WIDTH), F32),
        vm((2, 4, PB, WIDTH), BF16), vm((2, 4, PB, WIDTH), BF16),
        vm((2, 4, NY, PA, WIDTH), BF16), vm((2, 4, NY, PA, WIDTH), BF16),
        vm((2, PA, 512), BF16), vm((2, PA, 512), BF16),
        vm((2, PA, WIDTH), BF16), vm((2, PA, WIDTH), BF16),
        vm((2, HEADS, *state), F32),
        vm((2, 4, *state), BF16), vm((2, 4, *state), BF16),
        vm((2, CHIPS, 16, HDIM), BF16), vm((2, CHIPS, 16, HDIM), BF16),
        vm((2, CHIPS, 16, HDIM), BF16), vm((2, CHIPS, 16, HDIM), BF16),
        vm((2, 4, *state), BF16), vm((2, HEADS, *state), BF16),
        pltpu.SemaphoreType.REGULAR,
        dma((5,)), dma((2, 2)), dma((2, 2)),
        dma((2, 2, 4)), dma((2, 2, 8)), dma((2, 2, 8)),
        dma((2, 2)), dma((2, 2)), dma((2, 4, 2, 4)),
        dma((2, 8)), dma((2, 4, 2)), dma((2, 2)),
        dma((2, 2, 8)), dma((2, 2, 8)), dma((2, 2, 4)), dma((2, 2, 2, 4)),
        dma((2, 2)), dma((2, 2)),
        dma((2, 2)), dma((2, 2)), dma((2, 2)), dma((2, 2)),
    ]
    grad = jax.ShapeDtypeStruct((BLK, WIDTH), BF16)
    shapes = (grad, grad, grad, jax.ShapeDtypeStruct((ROWS, WIDTH), F32))
    far = pl.BlockSpec(memory_space=pltpu.HBM)
    close = pl.BlockSpec(memory_space=pltpu.VMEM)
    ins = [
        pltpu.with_memory_space_constraint(a, pltpu.HBM)
        for a in (query_act, key_act, value_act, out_weight, out_cotangent)
    ]
    made = pl.pallas_call(
        kernel,
        out_shape=shapes,
        in_specs=[far] * 5,
        out_specs=[close] * 4,
        scratch_shapes=scratch,
        compiler_params=pltpu.CompilerParams(
            collective_id=0, has_side_effects=True, vmem_limit_bytes=48 * 1024 * 1024
        ),
        name="layer_backward",
    )(*ins)
    return pl.pallas_call(
        handed_out,
        out_shape=shapes,
        in_specs=[close] * 4,
        out_specs=[far] * 4,
        scratch_shapes=[dma((4,))],
        compiler_params=pltpu.CompilerParams(vmem_limit_bytes=4 * 1024 * 1024),
        name="hand_out",
    )(*made)


def solution(mesh):
    finer = Mesh(mesh.devices.reshape(NZ, NY, NC, NX), ("z", "y", "c", "x"))
    spec = P(("z", "y", "c"), "x")
    return jax.shard_map(
        body, mesh=finer, in_specs=(spec,) * 5, out_specs=(spec,) * 4, check_vma=False
    )
```

```python
import functools

import jax
import jax.numpy as jnp
from jax import lax
from jax.experimental import pallas as pl
from jax.experimental.pallas import tpu as pltpu
from jax.sharding import Mesh
from jax.sharding import PartitionSpec as P

HDIM = 128
BLK = 256
EPS = 1e-06
NZ, NY, NC, NX = 8, 4, 2, 4
CHIPS = NZ * NY
HEADS = 8
ROWS = 48
WIDTH = 1024
COLS = 768
SLAB = NY * NC * ROWS
PA = 16
PB = 32
F32 = jnp.float32
BF16 = jnp.bfloat16
GRADW_SCALE = 1.0 / 128.0


def dot_nn(a, b):
    return lax.dot_general(a, b, (((1,), (0,)), ((), ())), preferred_element_type=F32)


def dot_nt(a, b):
    return lax.dot_general(a, b, (((1,), (1,)), ((), ())), preferred_element_type=F32)


def dot_tn(a, b):
    return lax.dot_general(a, b, (((0,), (0,)), ((), ())), preferred_element_type=F32)


def kernel(
    q_hbm, k_hbm, v_hbm, w_hbm, cot_hbm,
    gq, gk, gv, gw,
    q, k, v, wb, cot, cot_t, cot_o, normed, scores, raw, inv, da, draw, pk, pv,
    part, st1, r1, st2, r2, red, zst, zr, qst, qr, qy1s, qy1r, qy2s, qy2r,
    own, s_send, s_recv, a_send, a_recv, c_send, c_recv, e_send, e_recv,
    line_sem, load_sem, cx1, cx2, zp_sem, yp1, yp2, qy1, qy2, zq, sib, tsib, nsib,
    ry1, ry2, rz, qz, qya, qyb, ss, sa, sc, se,
):
    z, y, c, x = (lax.axis_index(n) for n in ("z", "y", "c", "x"))
    up_z, dn_z = lax.rem(z + 1, NZ), lax.rem(z + NZ - 1, NZ)
    up_y, dn_y, far_y = lax.rem(y + 1, NY), lax.rem(y + 3, NY), lax.rem(y + 2, NY)
    up_x, dn_x, far_x = lax.rem(x + 1, NX), lax.rem(x + 3, NX), lax.rem(x + 2, NX)
    other = 1 - c
    zdir = ({"z": up_z}, {"z": dn_z})
    ydir = ({"y": up_y}, {"y": dn_y})
    xdir = ({"x": up_x}, {"x": dn_x})
    pending = []

    def send(src, dst, sems, at, device):
        copy = pltpu.make_async_remote_copy(
            src_ref=src, dst_ref=dst, send_sem=sems.at[(0, *at)], recv_sem=sems.at[(1, *at)],
            device_id=device, device_id_type=pl.DeviceIdType.MESH,
        )
        copy.start()
        pending.append(copy)
        return copy

    loads = [
        pltpu.make_async_copy(src, dst, load_sem.at[i])
        for i, (src, dst) in enumerate(
            ((cot_hbm, cot.at[x]), (w_hbm, wb.at[z, y, c]), (k_hbm, k), (v_hbm, v), (q_hbm, q))
        )
    ]
    for load in loads:
        load.start()

    chip = z * NY + y

    def chip_peer(o):
        t = lax.rem(chip + o, CHIPS)
        return t, {"z": lax.div(t, NY), "y": lax.rem(t, NY)}

    barrier = pltpu.get_barrier_semaphore()

    def greet(peer):
        pl.semaphore_signal(barrier, inc=1, device_id=peer, device_id_type=pl.DeviceIdType.MESH)

    near = [{"c": other}, *xdir]
    near += [{"y": lax.rem(y + o, NY)} for o in range(1, NY)]
    near += [{"z": lax.rem(z + o, NZ)} for o in range(1, NZ)]
    for peer in near:
        greet(peer)

    def cols_of(h):
        return pl.ds(pl.multiple_of(h * HDIM, HDIM), HDIM)

    def for_heads(first, count, fn, unroll=2):
        @pl.loop(0, count // unroll)
        def _(i):
            for u in range(unroll):
                fn(first + i * unroll + u)

    mask = (
        lax.broadcasted_iota(jnp.int32, (BLK, BLK), 0)
        >= lax.broadcasted_iota(jnp.int32, (BLK, BLK), 1)
    )

    def kv_head(h):
        cs = cols_of(h)
        own[0, h] = dot_tn(k[:, cs], v[:, cs])

    def score_head(h):
        cs = cols_of(h)
        s = jnp.where(mask, dot_nt(q[:, cs], k[:, cs]), 0.0).astype(BF16)
        scores[h] = s
        raw[:, cs] = dot_nn(s, v[:, cs])

    def norm_head(h):
        cs = cols_of(h)
        r = raw[:, cs] + dot_nn(q[:, cs], e_recv[0, h])
        i = lax.rsqrt(jnp.mean(r * r, axis=-1, keepdims=True) + EPS)
        a = r * i
        raw[:, cs] = a
        inv[h] = i
        normed[0:BLK, cs] = a.astype(BF16)

    def draw_head(h):
        cs = cols_of(h)
        d, a = da[:, cs], raw[:, cs]
        center = jnp.mean(d * a, axis=-1, keepdims=True)
        dr = (inv[h] * (d - a * center)).astype(BF16)
        draw[:, cs] = dr
        own[1, h] = dot_tn(q[:, cs], dr)

    def local_grad_head(h):
        cs = cols_of(h)
        dr = draw[:, cs]
        ds = jnp.where(mask, dot_nt(dr, v[:, cs]), 0.0).astype(BF16)
        gq[:, cs] = (dot_nn(ds, k[:, cs]) + dot_nt(dr, e_recv[0, h])).astype(BF16)
        pk[:, cs] = dot_tn(ds, q[:, cs])
        pv[:, cs] = dot_tn(scores[h], dr)

    def final_grad_head(h):
        cs = cols_of(h)
        gk[:, cs] = (pk[:, cs] + dot_nt(v[:, cs], e_recv[1, h])).astype(BF16)
        gv[:, cs] = (pv[:, cs] + dot_nn(k[:, cs], e_recv[1, h])).astype(BF16)

    for i in (2, 3):
        loads[i].wait()
    for_heads(0, 8, kv_head, 8)
    loads[4].wait()
    for_heads(0, 8, score_head, 8)
    pl.semaphore_wait(barrier, len(near))
    for o in range(1, NY):
        dev = {"y": lax.rem(y + o, NY)}
        pl.semaphore_signal(line_sem, inc=1, device_id=dev, device_id_type=pl.DeviceIdType.MESH)

    loads[0].wait()
    cot1 = [send(cot.at[x], cot.at[x], cx1, (d,), xdir[d]) for d in (0, 1)]
    cot2 = []

    def cot_forward():
        cot1[0].wait_recv()
        half = cot.at[dn_x, pl.ds(0, 128)]
        cot2.append(send(half, half, cx2, (0,), xdir[0]))
        cot1[1].wait_recv()
        half = cot.at[up_x, pl.ds(128, 128)]
        cot2.append(send(half, half, cx2, (1,), xdir[1]))

    ag_z = [lax.rem(z + NZ + o, NZ) for o in (0, -1, 1, -2, 2, -3, 3, 4)]
    zp_c, yp1_c, yp2_c, qy1_c, qy2_c, zq_c, sib_c = {}, {}, {}, {}, {}, {}, {}

    def send_zp(r):
        for d, org in ((0, lax.rem(z + NZ - r, NZ)), (1, lax.rem(z + r, NZ))):
            rows = pl.ds(0, PB) if r < 3 else pl.ds(PA * d, PA)
            blk = wb.at[org, y, c, rows]
            zp_c[d, r] = send(blk, blk, zp_sem, (d, r), zdir[d])

    def send_yp1(i):
        for d in (0, 1):
            blk = wb.at[ag_z[i], y, c, pl.ds(0, PB)]
            yp1_c[d, i] = send(blk, blk, yp1, (d, i), ydir[d])

    def forward_yp(i):
        for d, org in ((0, dn_y), (1, up_y)):
            yp1_c[d, i].wait_recv()
            blk = wb.at[ag_z[i], org, c, pl.ds(PA * d, PA)]
            yp2_c[d, i] = send(blk, blk, yp2, (d, i), ydir[d])

    def send_qy1():
        for d in (0, 1):
            blk = wb.at[z, y, c, pl.ds(PB, PA)]
            qy1_c[d] = send(blk, blk, qy1, (d,), ydir[d])

    def forward_qy():
        for d, org in ((0, dn_y), (1, up_y)):
            qy1_c[d].wait_recv()
            blk = wb.at[z, org, c, pl.ds(PB, PA), pl.ds(512 * d, 512)]
            qy2_c[d] = send(blk, blk, qy2, (d,), ydir[d])

    q_rows = (y, dn_y, up_y, far_y)

    def send_zq(b, r):
        if r > 0:
            for d in (0, 1):
                zq_c[b, d, r - 1].wait_recv()
        for d, org in ((0, lax.rem(z + NZ - r, NZ)), (1, lax.rem(z + r, NZ))):
            lanes = pl.ds(0, WIDTH) if r < 3 else pl.ds(512 * d, 512)
            blk = wb.at[org, q_rows[b], c, pl.ds(PB, PA), lanes]
            zq_c[b, d, r] = send(blk, blk, zq, (b, d, r), zdir[d])

    def recv_both(copies, r):
        for d in (0, 1):
            copies[d, r].wait_recv()

    def ag_start():
        send_zp(0)
        send_qy1()
        send_zq(0, 0)
        send_yp1(0)

    def ag_q1():
        forward_qy()
        send_zq(1, 0)
        send_zq(2, 0)

    def ag_q2():
        qy2_c[0].wait_recv()
        qy2_c[1].wait_recv()
        send_zq(3, 0)

    def ag_p(r):
        recv_both(zp_c, r - 1)
        if r < 4:
            send_zp(r)
            send_yp1(2 * r - 1)
            send_yp1(2 * r)
        else:
            send_yp1(7)

    def send_sib(i):
        recv_both(yp2_c, i)
        if i == 7:
            for b in range(4):
                zq_c[b, 0, 3].wait_recv()
                zq_c[b, 1, 3].wait_recv()
        blk = wb.at[ag_z[i], :, c]
        sib_c[i] = send(blk, blk, sib, (i,), {"c": other})

    order = (range(CHIPS), range(CHIPS - 1, -1, -1))
    s_c, e_c = {}, {}
    mine4, rest4 = pl.ds(c * 4, 4), pl.ds(other * 4, 4)
    state4 = (4, HDIM, HDIM)

    def spread(src, dst, sem, s):
        @pl.loop(1, CHIPS)
        def _(o):
            t, dev = chip_peer(o)
            pltpu.make_async_remote_copy(
                src_ref=src.at[s, t], dst_ref=dst.at[s, chip],
                send_sem=sem.at[0, s], recv_sem=sem.at[1, s],
                device_id=dev, device_id_type=pl.DeviceIdType.MESH,
            ).start()

        dst[s, chip] = src[s, chip]
        all_but_one = pl.ds(0, CHIPS - 1)
        whole = pltpu.make_async_remote_copy(
            src_ref=src.at[s, all_but_one], dst_ref=dst.at[s, all_but_one],
            send_sem=sem.at[0, s], recv_sem=sem.at[1, s],
            device_id=chip_peer(1)[1], device_id_type=pl.DeviceIdType.MESH,
        )
        pending.append(whole)
        return whole

    a_c, c_c = {}, {}

    def scan_start(s):
        s_send[s] = own[s, rest4].astype(BF16)
        s_c[s] = send(s_send.at[s], s_recv.at[s], ss, (s,), {"c": other})

    def scan_a(s):
        s_c[s].wait_recv()
        total = own[s, mine4] + s_recv[s].astype(F32)
        a_send[s] = total.astype(BF16).reshape(CHIPS, 16, HDIM)
        if s == 0:
            pl.semaphore_wait(line_sem, NY - 1)
        a_c[s] = spread(a_send, a_recv, sa, s)

    def scan_c(s):
        a_c[s].wait_recv()
        run = jnp.zeros((16, HDIM), F32)
        for t in order[s]:
            c_send[s, t] = run.astype(BF16)
            run = run + a_recv[s, t].astype(F32)
        c_c[s] = spread(c_send, c_recv, sc, s)

    def scan_e(s):
        c_c[s].wait_recv()
        first = c == s
        outer = c_recv[s].reshape(state4).astype(F32)
        after_own = outer + own[s, mine4]
        after_sib = outer + s_recv[s].astype(F32)
        e_send[s] = jnp.where(first, after_own, outer).astype(BF16)
        e_c[s] = send(e_send.at[s], e_recv.at[s, mine4], se, (s,), {"c": other})
        e_recv[s, mine4] = jnp.where(first, outer, after_sib).astype(BF16)

    def scan_end(s):
        e_c[s].wait_recv()

    x_order = (x, dn_x, up_x, far_x)
    tsib_c = {}

    def turn(i):
        xo = x_order[i]
        for half in (0, 1):
            far_first = lax.rem(xo * 2 + half - z + NZ, NZ)
            zi = jnp.where(far_first < 4, 7 - 2 * far_first, 2 * far_first - 8)
            t = cot[xo, :, pl.ds(half * SLAB, SLAB)].T.reshape(NY, NC, ROWS, BLK)
            for yt in range(NY):
                dy = lax.rem(yt - y + NY, NY)
                yi = jnp.where(dy == 0, 3, jnp.where(dy == 2, 0, jnp.where(dy == 1, 1, 2)))
                keep = jnp.where(c == 0, t[yt, 0], t[yt, 1])
                give = jnp.where(c == 0, t[yt, 1], t[yt, 0])
                cot_t[zi, yi, :, 0:BLK] = keep
                cot_o[zi, yi] = give
            tsib_c[i, half] = send(
                cot_o.at[zi], cot_t.at[zi, :, :, pl.ds(BLK, BLK)], tsib, (i, half), {"c": other}
            )

    def d_attn(idx, first=False):
        for i in idx:
            sib_c[i].wait_recv()

        lhs, rhs = [], []
        for i in idx:
            zo = ag_z[i]
            lanes = pl.ds(pl.multiple_of(lax.rem(zo, 2) * SLAB, 128), SLAB)
            lhs.append(cot[lax.div(zo, 2), :, lanes])
            rhs.append(wb[zo].reshape(SLAB, WIDTH))
        t = dot_nn(jnp.concatenate(lhs, 1), jnp.concatenate(rhs, 0))
        da[...] = t if first else da[...] + t

    up_of, dn_of = (0, 1, 3, 5), (0, 2, 4, 6)
    y_of = (1, 2)
    ry1_c, ry2_c, rz_c, qz_c, qya_c, qyb_c = {}, {}, {}, {}, {}, {}

    def product(lo, hi):
        n = hi - lo

        acc = dot_nn(cot_t[lo:hi].reshape(n * NY * ROWS, 2 * BLK), normed[...])
        part[lo:hi] = acc.reshape(n, NY, ROWS, WIDTH)

    def step1(i):
        st1[i] = part[i, 0, 0:PB].astype(BF16)
        for d in (0, 1):
            ry1_c[d, i] = send(st1.at[i, pl.ds(PA * d, PA)], r1.at[d, i], ry1, (d, i), ydir[d])

    def step2(i):
        for d in (0, 1):
            t = y_of[d]
            ry1_c[d, i].wait_recv()
            mine, rest = slice(PA * d, PA * d + PA), slice(PA - PA * d, PB - PA * d)
            st2[d, i, mine] = (part[i, t, mine] + r1[d, i].astype(F32)).astype(BF16)
            st2[d, i, rest] = part[i, t, rest].astype(BF16)
            ry2_c[d, i] = send(st2.at[d, i], r2.at[d, i], ry2, (d, i), ydir[d])

    def step3(i):
        recv_both(ry2_c, i)
        red[i] = part[i, 3, 0:PB] + (r2[0, i].astype(F32) + r2[1, i].astype(F32))

    def chain(s):
        for d, idx in ((0, up_of), (1, dn_of)):
            i = idx[s]
            mine = slice(PA * d, PA * d + PA)
            if s == 0:
                zst[d, 0, mine] = red[i, mine].astype(BF16)
                blk = pl.ds(PA * d, PA)
                rz_c[d, s] = send(zst.at[d, 0, blk], zr.at[d, 0, blk], rz, (d, s), zdir[d])
                continue
            rz_c[d, s - 1].wait_recv()
            if s == 1:
                rest = slice(PA - PA * d, PB - PA * d)
                zst[d, s, mine] = (red[i, mine] + zr[d, 0, mine].astype(F32)).astype(BF16)
                zst[d, s, rest] = red[i, rest].astype(BF16)
            else:
                zst[d, s] = (red[i] + zr[d, s - 1].astype(F32)).astype(BF16)
            rz_c[d, s] = send(zst.at[d, s], zr.at[d, s], rz, (d, s), zdir[d])

    def chain_end():
        recv_both(rz_c, 3)
        total = red[7] + (zr[0, 3].astype(F32) + zr[1, 3].astype(F32))
        gw[0:PB] = total * GRADW_SCALE

    def qchain(b, s):
        ys = pl.ds(2 * b, 2)
        for d, idx in ((0, up_of), (1, dn_of)):
            i = idx[s]
            term = part[i, 2 * b : 2 * b + 2, PB:ROWS]
            if s > 0:
                qz_c[b, d, s - 1].wait_recv()
            if s == 0:
                t = 2 * b + d
                qst[d, 0, t] = part[i, t, PB:ROWS].astype(BF16)
                blk = pl.ds(t, 1)
                qz_c[b, d, s] = send(qst.at[d, 0, blk], qr.at[d, 0, blk], qz, (b, d, s), zdir[d])
                continue
            if s == 1:
                t, u = 2 * b + d, 2 * b + 1 - d
                qst[d, s, t] = (part[i, t, PB:ROWS] + qr[d, 0, t].astype(F32)).astype(BF16)
                qst[d, s, u] = part[i, u, PB:ROWS].astype(BF16)
            else:
                got = qr[d, s - 1, 2 * b : 2 * b + 2].astype(F32)
                qst[d, s, 2 * b : 2 * b + 2] = (term + got).astype(BF16)
            qz_c[b, d, s] = send(qst.at[d, s, ys], qr.at[d, s, ys], qz, (b, d, s), zdir[d])

    def q_sum(b):
        for d in (0, 1):
            qz_c[b, d, 3].wait_recv()
        ys = slice(2 * b, 2 * b + 2)
        got = qr[0, 3, ys].astype(F32) + qr[1, 3, ys].astype(F32)
        part[7, ys, PB:ROWS] = part[7, ys, PB:ROWS] + got

    def q_y1():
        q_sum(0)
        for d in (0, 1):
            qy1s[d] = part[7, 0, PB:ROWS, 512 * d : 512 * d + 512].astype(BF16)
            qya_c[d] = send(qy1s.at[d], qy1r.at[d], qya, (d,), ydir[d])

    def q_y2():
        q_sum(1)
        for d in (0, 1):
            t = y_of[d]
            qya_c[d].wait_recv()
            mine = slice(512 * d, 512 * d + 512)
            rest = slice(512 - 512 * d, 1024 - 512 * d)
            qy2s[d, :, mine] = (part[7, t, PB:ROWS, mine] + qy1r[d].astype(F32)).astype(BF16)
            qy2s[d, :, rest] = part[7, t, PB:ROWS, rest].astype(BF16)
            qyb_c[d] = send(qy2s.at[d], qy2r.at[d], qyb, (d,), ydir[d])

    def q_end():
        for d in (0, 1):
            qyb_c[d].wait_recv()
        total = part[7, 3, PB:ROWS] + (qy2r[0].astype(F32) + qy2r[1].astype(F32))
        gw[PB:ROWS] = total * GRADW_SCALE

    half8 = ((0, 4), (4, 4))
    nsib_c = []

    def norm(n):
        part8 = (c, other)[n]
        for_heads(part8 * 4, 4, norm_head, 4)
        blk = pl.ds(pl.multiple_of(part8 * 512, 512), 512)
        src, dst = normed.at[pl.ds(0, BLK), blk], normed.at[pl.ds(BLK, BLK), blk]
        nsib_c.append(send(src, dst, nsib, (n,), {"c": other}))

    def cot_wait():
        for copy in cot2:
            copy.wait_recv()

    def sib_wait():
        for copy in nsib_c:
            copy.wait_recv()
        for copy in tsib_c.values():
            copy.wait_recv()

    def local_grad(n):
        for_heads(*half8[n], local_grad_head, 4)

    def final_grad(n):
        for_heads((c, other)[n] * 4, 4, final_grad_head, 4)

    loads[1].wait()
    ag_start()
    scan_start(0)
    turn(0)
    scan_a(0)
    ag_q1()
    ag_p(1)
    send_zq(0, 1)
    forward_yp(0)
    ag_q2()
    forward_yp(1)
    send_zq(1, 1)
    send_zq(2, 1)
    forward_yp(2)
    scan_c(0)
    send_sib(0)
    ag_p(2)
    cot_forward()
    turn(1)
    send_zq(3, 1)
    send_sib(1)
    turn(2)
    send_sib(2)
    send_zq(1, 2)
    send_zq(2, 2)
    send_zq(0, 2)
    forward_yp(3)
    forward_yp(4)
    ag_p(3)
    cot_wait()
    d_attn((0, 1, 2), True)
    scan_e(0)
    norm(0)
    send_zq(1, 3)
    send_zq(3, 2)
    send_sib(3)
    turn(3)
    send_zq(0, 3)
    scan_end(0)
    ag_p(4)
    norm(1)
    forward_yp(5)
    send_sib(4)
    send_zq(2, 3)
    send_zq(3, 3)
    forward_yp(6)
    sib_wait()
    product(0, 1)
    step1(0)
    qchain(0, 0)
    qchain(1, 0)
    d_attn((3, 4))
    forward_yp(7)
    product(1, 3)
    send_sib(5)
    step1(2)
    step1(1)
    send_sib(6)
    product(3, 5)
    step2(0)
    qchain(0, 1)
    step1(3)
    step1(4)
    send_sib(7)
    qchain(1, 1)
    product(5, 8)
    step2(2)
    step1(6)
    d_attn((5, 6))
    d_attn((7,))
    for_heads(0, 8, draw_head, 8)
    scan_start(1)
    qchain(0, 2)
    step3(0)
    chain(0)
    step2(1)
    step2(4)
    scan_a(1)
    qchain(1, 2)
    step2(3)
    step3(2)
    step1(5)
    local_grad(0)
    local_grad(1)
    qchain(0, 3)
    step3(1)
    chain(1)
    step2(6)
    step1(7)
    step3(4)
    qchain(1, 3)
    step3(3)
    step2(5)
    scan_c(1)
    q_y1()
    step3(6)
    chain(2)
    step2(7)
    step3(5)
    q_y2()
    step3(7)
    chain(3)
    scan_e(1)
    final_grad(0)
    q_end()
    scan_end(1)
    final_grad(1)
    chain_end()
    for copy in pending:
        copy.wait_send()


def handed_out(*refs):
    ins, outs, sems = refs[:4], refs[4:8], refs[8]
    copies = [pltpu.make_async_copy(a, b, sems.at[i]) for i, (a, b) in enumerate(zip(ins, outs))]
    for copy in copies:
        copy.start()
    for copy in copies:
        copy.wait()


def body(query_act, key_act, value_act, out_weight, out_cotangent):
    vm = pltpu.VMEM
    dma = pltpu.SemaphoreType.DMA
    state = (HDIM, HDIM)
    scratch = [
        vm((BLK, WIDTH), BF16), vm((BLK, WIDTH), BF16), vm((BLK, WIDTH), BF16),
        vm((NZ, NY, NC, ROWS, WIDTH), BF16),
        vm((NX, BLK, COLS), BF16),
        vm((NZ, NY, ROWS, 2 * BLK), BF16), vm((NZ, NY, ROWS, BLK), BF16),
        vm((2 * BLK, WIDTH), BF16),
        vm((HEADS, BLK, BLK), BF16),
        vm((BLK, WIDTH), F32),
        vm((HEADS, BLK, 1), F32),
        vm((BLK, WIDTH), F32),
        vm((BLK, WIDTH), BF16),
        vm((BLK, WIDTH), F32), vm((BLK, WIDTH), F32),
        vm((NZ, NY, ROWS, WIDTH), F32),
        vm((8, PB, WIDTH), BF16), vm((2, 8, PA, WIDTH), BF16),
        vm((2, 8, PB, WIDTH), BF16), vm((2, 8, PB, WIDTH), BF16),
        vm((8, PB, WIDTH), F32),
        vm((2, 4, PB, WIDTH), BF16), vm((2, 4, PB, WIDTH), BF16),
        vm((2, 4, NY, PA, WIDTH), BF16), vm((2, 4, NY, PA, WIDTH), BF16),
        vm((2, PA, 512), BF16), vm((2, PA, 512), BF16),
        vm((2, PA, WIDTH), BF16), vm((2, PA, WIDTH), BF16),
        vm((2, HEADS, *state), F32),
        vm((2, 4, *state), BF16), vm((2, 4, *state), BF16),
        vm((2, CHIPS, 16, HDIM), BF16), vm((2, CHIPS, 16, HDIM), BF16),
        vm((2, CHIPS, 16, HDIM), BF16), vm((2, CHIPS, 16, HDIM), BF16),
        vm((2, 4, *state), BF16), vm((2, HEADS, *state), BF16),
        pltpu.SemaphoreType.REGULAR,
        dma((5,)), dma((2, 2)), dma((2, 2)),
        dma((2, 2, 4)), dma((2, 2, 8)), dma((2, 2, 8)),
        dma((2, 2)), dma((2, 2)), dma((2, 4, 2, 4)),
        dma((2, 8)), dma((2, 4, 2)), dma((2, 2)),
        dma((2, 2, 8)), dma((2, 2, 8)), dma((2, 2, 4)), dma((2, 2, 2, 4)),
        dma((2, 2)), dma((2, 2)),
        dma((2, 2)), dma((2, 2)), dma((2, 2)), dma((2, 2)),
    ]
    grad = jax.ShapeDtypeStruct((BLK, WIDTH), BF16)
    shapes = (grad, grad, grad, jax.ShapeDtypeStruct((ROWS, WIDTH), F32))
    far = pl.BlockSpec(memory_space=pltpu.HBM)
    close = pl.BlockSpec(memory_space=pltpu.VMEM)
    ins = [
        pltpu.with_memory_space_constraint(a, pltpu.HBM)
        for a in (query_act, key_act, value_act, out_weight, out_cotangent)
    ]
    made = pl.pallas_call(
        kernel,
        out_shape=shapes,
        in_specs=[far] * 5,
        out_specs=[close] * 4,
        scratch_shapes=scratch,
        compiler_params=pltpu.CompilerParams(
            collective_id=0, has_side_effects=True, vmem_limit_bytes=48 * 1024 * 1024
        ),
        name="layer_backward",
    )(*ins)
    return pl.pallas_call(
        handed_out,
        out_shape=shapes,
        in_specs=[close] * 4,
        out_specs=[far] * 4,
        scratch_shapes=[dma((4,))],
        compiler_params=pltpu.CompilerParams(vmem_limit_bytes=4 * 1024 * 1024),
        name="hand_out",
    )(*made)


def solution(mesh):
    finer = Mesh(mesh.devices.reshape(NZ, NY, NC, NX), ("z", "y", "c", "x"))
    spec = P(("z", "y", "c"), "x")
    return jax.shard_map(
        body, mesh=finer, in_specs=(spec,) * 5, out_specs=(spec,) * 4, check_vma=False
    )
```
